512 devices in a mesh: ctx: 32 (over y, x, core), tp: 16 (over z).
Axes of the slice: x: 4, y: 4, z: 16, core: 2. Of those that a mesh axis runs over, the one named last changes fastest.
Arguments:
- features: bfloat16 [8192, 3, 4096], P('ctx', None, 'tp'), may hold values from -6 to 6
- short_taps: float32 [3, 3, 4096], P(None, None, 'tp'), may hold values from -3.5 to 3.5
- residues: float32 [16, 256], P(None, 'tp'), may hold values from -1.5 to 1.5
- rates: float32 [16, 256], P(None, 'tp'), may hold values from 3.6621094e-05 to 0.05, as said below
- skip: float32 [4096], P('tp'), may hold values from -4 to 4
- out_weight: bfloat16 [4096, 4096], P(None, 'tp'), may hold values from -0.09375 to 0.09375
Outputs:
- mixed: bfloat16 [8192, 4096], P('ctx', 'tp')
The draws below stay inside these ranges and needn't reach their ends.
Inputs may be any that keep to these rules, and one draw needn't show every extreme that they name: `rates`: decay rate of one mode of one filter.
All inputs are finite; a program needn't handle non-finite values.
Results may differ from the reference program's by a relative error of at most 0.0049.
Values may be sent and summed in bfloat16 or wider, within the bound.
No kernel may reach another device: no remote copies, remote signals or barrier semaphores. Data moves between devices by JAX's collectives and lax.ppermute only.
A program may use at most 128 MiB of HBM per device.

```python
import jax
import jax.numpy as jnp
from jax import lax

D = 4096
GROUP = 16
ORDER = 16
SHORT = 3
SEQ = 8192
FILTERS = 256


def draw_rates(key, part):
    uniform_part = jax.random.uniform(key, (ORDER, FILTERS), jnp.float32)
    lowest = 0.3 / SEQ
    highest = 0.05
    return jnp.exp(jnp.log(lowest) + uniform_part * (jnp.log(highest) - jnp.log(lowest)))


def steps_of(own_key, dims, shards, low, largest):
    level, own = 1.0, jax.random.fold_in(own_key, 6)
    for dim, shards_of in shards:
        steps = jnp.exp(jax.random.uniform(jax.random.fold_in(own, dim), (shards_of,), jnp.float32, low / len(shards), largest / len(shards)))
        level = level * jnp.repeat(steps, dims[dim] // shards_of).reshape([-1 if axis == dim else 1 for axis in range(len(dims))])
    return level


def scatter_about(stream_key, shape, scale, most, cuts=(), held_as=jnp.bfloat16):
    gain = steps_of(stream_key, shape, cuts, -0.22, 0.18) if cuts else 1.0
    array = jax.random.normal(stream_key, shape, jnp.float32) * scale * gain
    return jnp.minimum(jnp.maximum(array, -most), most).astype(held_as)


def setup_inputs(seed: int = 0) -> dict:
    seeds = jax.random.split(jax.random.key(seed), 7)
    features = scatter_about(seeds[0], (SEQ, 3, D), 1.0, 6.0, ((0, 32), (2, 16)))
    short_taps = scatter_about(seeds[1], (SHORT, 3, D), SHORT ** -0.5, 3.5, ((2, 16),), jnp.float32)
    residues = scatter_about(seeds[2], (ORDER, FILTERS), ORDER ** -0.5, 1.5, ((1, 16),), jnp.float32)
    rates = draw_rates(jax.random.fold_in(seeds[6], 71), 0)
    skip = scatter_about(seeds[4], (D,), 1.0, 4.0, ((0, 16),), jnp.float32)
    out_weight = scatter_about(seeds[5], (D, D), D ** -0.5, 0.09375, ((1, 16),))
    return dict(features=features, short_taps=short_taps, residues=residues, rates=rates, skip=skip, out_weight=out_weight)


column_block = 256

def short_filter(feats, taps):
    lead = jnp.zeros((SHORT - 1,) + feats.shape[1:], feats.dtype)
    extended = jnp.concatenate([lead, feats], 0)
    total = jnp.zeros(feats.shape, jnp.float32)
    for shift in range(SHORT):
        window = extended[SHORT - 1 - shift:SHORT - 1 - shift + SEQ].astype(jnp.float32)
        total = total + taps[shift] * window
    return total

def channel_block(pieces):
    feats, taps, skip_part, filt_part = pieces
    shorted = short_filter(feats, taps)
    query = shorted[:, 0, :]
    product = shorted[:, 1, :] * shorted[:, 2, :]
    spectrum = jnp.fft.rfft(product, n=2 * SEQ, axis=0) * jnp.fft.rfft(filt_part, n=2 * SEQ, axis=0)
    conv = jnp.fft.irfft(spectrum, n=2 * SEQ, axis=0)[:SEQ]
    return (query * (conv + skip_part * product)).astype(jnp.bfloat16)

def reference(features, short_taps, residues, rates, skip, out_weight):
    block_count = D // column_block
    positions = jnp.arange(SEQ).astype(jnp.float32)[:, None]
    filt = jnp.zeros((SEQ, FILTERS), jnp.float32)
    for order in range(ORDER):
        filt = filt + residues[order] * jnp.sqrt(2.0 * rates[order]) * jnp.exp(-rates[order] * positions)
    filt_full = jnp.repeat(filt, GROUP, axis=1)
    feats_blocks = features.reshape(SEQ, 3, block_count, column_block).transpose(2, 0, 1, 3)
    taps_blocks = short_taps.reshape(SHORT, 3, block_count, column_block).transpose(2, 0, 1, 3)
    skip_blocks = skip.reshape(block_count, column_block)
    filt_blocks = filt_full.reshape(SEQ, block_count, column_block).transpose(1, 0, 2)
    gated = lax.map(channel_block, (feats_blocks, taps_blocks, skip_blocks, filt_blocks))
    gated = gated.transpose(1, 0, 2).reshape(SEQ, D)
    return jnp.dot(gated, out_weight, preferred_element_type=jnp.float32).astype(jnp.bfloat16)
```

```python
import functools

import jax
import jax.numpy as jnp
from jax import lax
from jax.experimental import pallas as pl
from jax.experimental.pallas import tpu as pltpu
from jax.sharding import PartitionSpec as P

SHORT = 3
CHUNKS = 8
RIM = 16
LANES = 128
HIGHEST = lax.Precision.HIGHEST


def per_channel(table, width):
    filters = table.shape[1]
    group = width // filters
    row = lax.broadcasted_iota(jnp.int32, (filters, width), 0)
    col = lax.broadcasted_iota(jnp.int32, (filters, width), 1)
    pick = jnp.where(col // group == row, 1.0, 0.0).astype(jnp.float32)
    return lax.dot_general(
        table, pick, (((1,), (0,)), ((), ())), precision=HIGHEST,
        preferred_element_type=jnp.float32,
    )


def short_filter(block, taps, before_last, last):
    row = lax.broadcasted_iota(jnp.int32, block.shape, 0)
    one = jnp.where(row == 0, last, pltpu.roll(block, 1, 0))
    two = jnp.where(row == 0, before_last, jnp.where(row == 1, last, pltpu.roll(block, 2, 0)))
    return taps[0] * block + taps[1] * one + taps[2] * two


def save(ref, array):
    rows, width = array.shape
    for t in range(width // LANES):
        ref[pl.ds(t * rows, rows), :] = array[:, t * LANES : (t + 1) * LANES]


def strided(ref, rows, width, start, count, stride):
    return jnp.concatenate(
        [ref[pl.ds(t * rows + start, count, stride=stride), :] for t in range(width // LANES)], 1
    )


def spread(table, r, t):
    return jnp.broadcast_to(table[r : r + 1, t * LANES : (t + 1) * LANES], (CHUNKS, LANES))


def recur(product_ref, base, decay, states, steps, visit=None):
    def step(i, carry):
        now = product_ref[pl.ds(base + i, CHUNKS, stride=steps), :]
        carry = tuple(d * h + now for d, h in zip(decay, carry))
        if visit is not None:
            visit(i, carry)
        return carry

    return lax.fori_loop(0, steps, step, states, unroll=4)


def chunk_ends(product_ref, ends_ref, lam, rows):
    modes, width = lam.shape
    decay = jnp.exp(-lam)
    for t in range(width // LANES):
        blank = tuple(jnp.zeros((CHUNKS, LANES), jnp.float32) for _ in range(modes))
        part = [spread(decay, r, t) for r in range(modes)]
        ends = recur(product_ref, t * rows, part, blank, rows // CHUNKS)
        for r, end in enumerate(ends):
            ends_ref[pl.ds((t * modes + r) * CHUNKS, CHUNKS), :] = end


def state_kernel(feat_ref, taps_ref, rates_ref, send_ref, product_ref, ends_ref):
    rows, width = feat_ref.shape[1:]
    modes = rates_ref.shape[0]
    lam = per_channel(rates_ref[...], width)
    zero = jnp.zeros((1, width), jnp.float32)
    keys, values = (
        short_filter(
            feat_ref[j].astype(jnp.float32), [taps_ref[s, j : j + 1, :] for s in range(SHORT)],
            zero, zero,
        )
        for j in (1, 2)
    )
    row = lax.broadcasted_iota(jnp.int32, (rows, width), 0)
    save(product_ref, jnp.where(row < SHORT - 1, 0.0, keys * values))
    chunk_ends(product_ref, ends_ref, lam, rows)
    over_chunk = jnp.exp(-lam * float(rows // CHUNKS))
    total = jnp.zeros((modes, width), jnp.float32)
    for j in range(CHUNKS):
        end = strided(ends_ref, modes * CHUNKS, width, j, modes, CHUNKS)
        total = total * over_chunk + end
    head = [feat_ref[j, 0:2, :].astype(jnp.float32) for j in (1, 2)]
    tail = [feat_ref[j, rows - 2 : rows, :].astype(jnp.float32) for j in (1, 2, 0)]
    rim = jnp.concatenate(head + tail + [jnp.zeros((RIM - 10, width), jnp.float32)], 0)
    block = jnp.concatenate([total, rim], 0).astype(jnp.bfloat16)
    for e in range(send_ref.shape[0]):
        send_ref[e] = block


def gate_kernel(
    recv_ref, feat_ref, taps_ref, rates_ref, residues_ref, skip_ref, out_ref,
    rims_ref, product_ref, states_ref, conv_ref,
):
    blocks = recv_ref.shape[0]
    rows, width = feat_ref.shape[1:]
    modes = rates_ref.shape[0]
    steps = rows // CHUNKS
    own = lax.axis_index("ctx")
    lam = per_channel(rates_ref[...], width)
    coef = per_channel(residues_ref[...] * jnp.sqrt(2.0 * rates_ref[...]), width)
    taps = [[taps_ref[s, j : j + 1, :] for s in range(SHORT)] for j in range(3)]

    for e in range(blocks):
        edges = recv_ref[e, pl.ds(modes, RIM), :].astype(jnp.float32)
        for t in range(width // LANES):
            rims_ref[pl.ds((t * blocks + e) * RIM, RIM), :] = edges[:, t * LANES : (t + 1) * LANES]

    def edge(k):
        return strided(rims_ref, blocks * RIM, width, k, blocks, RIM)

    block_row = lax.broadcasted_iota(jnp.int32, (blocks, width), 0)

    def earlier(k):
        return jnp.where(block_row == 0, 0.0, pltpu.roll(edge(k), 1, 0))

    def firsts(j, head, tail):
        zeroth, first = edge(head), edge(head + 1)
        before_last, last = earlier(tail), earlier(tail + 1)
        a, b, c = taps[j]
        return a * zeroth + b * last + c * before_last, a * first + b * zeroth + c * last

    key0, key1 = firsts(1, 0, 4)
    value0, value1 = firsts(2, 2, 6)
    product0, product1 = key0 * value0, key1 * value1

    over_block = jnp.exp(-lam * float(rows))
    weight0 = jnp.exp(-lam * float(rows - 1))
    weight1 = jnp.exp(-lam * float(rows - 2))
    state = jnp.zeros((modes, width), jnp.float32)
    for e in range(blocks - 1):
        added = (
            recv_ref[e, pl.ds(0, modes), :].astype(jnp.float32)
            + weight0 * product0[e : e + 1]
            + weight1 * product1[e : e + 1]
        )
        state = jnp.where(e < own, state * over_block + added, state)

    previous = jnp.maximum(own - 1, 0)
    tails = recv_ref[previous, pl.ds(modes, RIM), :].astype(jnp.float32)
    tails = jnp.where(own > 0, tails, 0.0)
    query, keys, values = (
        short_filter(
            feat_ref[j].astype(jnp.float32), taps[j], tails[k : k + 1], tails[k + 1 : k + 2]
        )
        for j, k in ((0, 8), (1, 4), (2, 6))
    )
    product = keys * values
    save(product_ref, product)

    chunk_ends(product_ref, states_ref, lam, rows)
    over_chunk = jnp.exp(-lam * float(steps))
    for j in range(CHUNKS):
        end = strided(states_ref, modes * CHUNKS, width, j, modes, CHUNKS)
        for t in range(width // LANES):
            where = pl.ds(t * modes * CHUNKS + j, modes, stride=CHUNKS)
            states_ref[where, :] = state[:, t * LANES : (t + 1) * LANES]
        state = state * over_chunk + end

    decay = jnp.exp(-lam)
    for t in range(width // LANES):
        part = [spread(decay, r, t) for r in range(modes)]
        scale = [spread(coef, r, t) for r in range(modes)]
        begin = tuple(
            states_ref[pl.ds((t * modes + r) * CHUNKS, CHUNKS), :] for r in range(modes)
        )

        def visit(i, carry, t=t, scale=scale):
            total = functools.reduce(jnp.add, [s * h for s, h in zip(scale, carry)])
            conv_ref[pl.ds(t * rows + i, CHUNKS, stride=steps), :] = total

        recur(product_ref, t * rows, part, begin, steps, visit)

    conv = jnp.concatenate(
        [conv_ref[pl.ds(t * rows, rows), :] for t in range(width // LANES)], 1
    )
    gated = query * (conv + skip_ref[...] * product)
    gated = gated.astype(jnp.bfloat16).astype(jnp.float32)
    root = jnp.sqrt(jnp.sqrt(jnp.abs(gated) * 2.0**32))
    out_ref[...] = jnp.where(gated < 0.0, -root, root)


def shards(features, short_taps, residues, rates, skip, out_weight):
    blocks = lax.axis_size("ctx")
    rows, _, width = features.shape
    modes = rates.shape[0]
    feats = features.transpose(1, 0, 2)
    f32 = jnp.float32
    tiles = width // LANES
    sent = pl.pallas_call(
        state_kernel,
        out_shape=jax.ShapeDtypeStruct((blocks, modes + RIM, width), jnp.bfloat16),
        scratch_shapes=[
            pltpu.VMEM((tiles * rows, LANES), f32),
            pltpu.VMEM((tiles * modes * CHUNKS, LANES), f32),
        ],
        name="block_state",
    )(feats, short_taps, rates)
    received = lax.all_to_all(sent, "ctx", split_axis=0, concat_axis=0, tiled=True)
    coded = pl.pallas_call(
        gate_kernel,
        out_shape=jax.ShapeDtypeStruct((rows, width), f32),
        scratch_shapes=[
            pltpu.VMEM((tiles * blocks * RIM, LANES), f32),
            pltpu.VMEM((tiles * rows, LANES), f32),
            pltpu.VMEM((tiles * modes * CHUNKS, LANES), f32),
            pltpu.VMEM((tiles * rows, LANES), f32),
        ],
        name="conv_gate",
    )(received, feats, short_taps, rates, residues, skip.reshape(1, width))
    gathered = lax.all_gather(coded.astype(jnp.float16), "tp", axis=1, tiled=True).astype(f32)
    square = gathered * gathered
    gated = (square * (gathered * jnp.abs(gathered)) * 2.0**-32).astype(jnp.bfloat16)
    return jnp.dot(gated, out_weight, preferred_element_type=f32).astype(jnp.bfloat16)


def solution(mesh):
    in_specs = (
        P("ctx", None, "tp"),
        P(None, None, "tp"),
        P(None, "tp"),
        P(None, "tp"),
        P("tp"),
        P(None, "tp"),
    )
    return jax.shard_map(
        shards, mesh=mesh, in_specs=in_specs, out_specs=P("ctx", "tp"), check_vma=False
    )
```

```python
import functools

import jax
import jax.numpy as jnp
from jax import lax
from jax.experimental import pallas as pl
from jax.experimental.pallas import tpu as pltpu
from jax.sharding import PartitionSpec as P

SHORT = 3
CHUNKS = 8
RIM = 16
LANES = 128
HIGHEST = lax.Precision.HIGHEST


def per_channel(table, width):
    filters = table.shape[1]
    group = width // filters
    row = lax.broadcasted_iota(jnp.int32, (filters, width), 0)
    col = lax.broadcasted_iota(jnp.int32, (filters, width), 1)
    pick = jnp.where(col // group == row, 1.0, 0.0).astype(jnp.float32)
    return lax.dot_general(
        table, pick, (((1,), (0,)), ((), ())), precision=HIGHEST,
        preferred_element_type=jnp.float32,
    )


def short_filter(block, taps, before_last, last):
    row = lax.broadcasted_iota(jnp.int32, block.shape, 0)
    one = jnp.where(row == 0, last, pltpu.roll(block, 1, 0))
    two = jnp.where(row == 0, before_last, jnp.where(row == 1, last, pltpu.roll(block, 2, 0)))
    return taps[0] * block + taps[1] * one + taps[2] * two


def save(ref, array):
    rows, width = array.shape
    for t in range(width // LANES):
        ref[pl.ds(t * rows, rows), :] = array[:, t * LANES : (t + 1) * LANES]


def strided(ref, rows, width, start, count, stride):
    return jnp.concatenate(
        [ref[pl.ds(t * rows + start, count, stride=stride), :] for t in range(width // LANES)], 1
    )


def whole(ref, rows, width):
    return jnp.concatenate([ref[pl.ds(t * rows, rows), :] for t in range(width // LANES)], 1)


def spread(table, r, t):
    return jnp.broadcast_to(table[r : r + 1, t * LANES : (t + 1) * LANES], (CHUNKS, LANES))


def recur(product_ref, base, decay, states, steps, visit=None):
    def step(i, carry):
        now = product_ref[pl.ds(base + i, CHUNKS, stride=steps), :]
        carry = tuple(d * h + now for d, h in zip(decay, carry))
        if visit is not None:
            visit(i, carry)
        return carry

    return lax.fori_loop(0, steps, step, states, unroll=4)


def chunk_ends(product_ref, ends_ref, lam, rows):
    modes, width = lam.shape
    decay = jnp.exp(-lam)
    for t in range(width // LANES):
        blank = tuple(jnp.zeros((CHUNKS, LANES), jnp.float32) for _ in range(modes))
        part = [spread(decay, r, t) for r in range(modes)]
        ends = recur(product_ref, t * rows, part, blank, rows // CHUNKS)
        for r, end in enumerate(ends):
            ends_ref[pl.ds((t * modes + r) * CHUNKS, CHUNKS), :] = end


def channel_taps(taps_ref, j):
    return [taps_ref[s, j : j + 1, :] for s in range(SHORT)]


def inner_product(feat_ref, taps_ref):
    rows, width = feat_ref.shape[1:]
    zero = jnp.zeros((1, width), jnp.float32)
    keys, values = (
        short_filter(feat_ref[j].astype(jnp.float32), channel_taps(taps_ref, j), zero, zero)
        for j in (1, 2)
    )
    row = lax.broadcasted_iota(jnp.int32, (rows, width), 0)
    return jnp.where(row < SHORT - 1, 0.0, keys * values)


def state_kernel(feat_ref, taps_ref, rates_ref, send_ref, product_ref, ends_ref):
    rows, width = feat_ref.shape[1:]
    modes = rates_ref.shape[0]
    lam = per_channel(rates_ref[...], width)
    save(product_ref, inner_product(feat_ref, taps_ref))
    chunk_ends(product_ref, ends_ref, lam, rows)
    over_chunk = jnp.exp(-lam * float(rows // CHUNKS))
    total = jnp.zeros((modes, width), jnp.float32)
    for j in range(CHUNKS):
        end = strided(ends_ref, modes * CHUNKS, width, j, modes, CHUNKS)
        total = total * over_chunk + end
    head = [feat_ref[j, 0:2, :].astype(jnp.float32) for j in (1, 2)]
    tail = [feat_ref[j, rows - 2 : rows, :].astype(jnp.float32) for j in (1, 2, 0)]
    own_query = [feat_ref[0, 0:2, :].astype(jnp.float32)]
    blank = [jnp.zeros((RIM - 12, width), jnp.float32)]
    rim = jnp.concatenate(head + tail + own_query + blank, 0)
    block = jnp.concatenate([total, rim], 0).astype(jnp.bfloat16)
    for e in range(send_ref.shape[0]):
        send_ref[e] = block


def local_kernel(
    feat_ref, taps_ref, rates_ref, residues_ref, skip_ref, query_ref, base_ref,
    product_ref, states_ref, conv_ref,
):
    rows, width = feat_ref.shape[1:]
    modes = rates_ref.shape[0]
    steps = rows // CHUNKS
    lam = per_channel(rates_ref[...], width)
    coef = per_channel(residues_ref[...] * jnp.sqrt(2.0 * rates_ref[...]), width)
    zero = jnp.zeros((1, width), jnp.float32)
    query = short_filter(feat_ref[0].astype(jnp.float32), channel_taps(taps_ref, 0), zero, zero)
    product = inner_product(feat_ref, taps_ref)
    save(product_ref, product)
    chunk_ends(product_ref, states_ref, lam, rows)
    over_chunk = jnp.exp(-lam * float(steps))
    state = jnp.zeros((modes, width), jnp.float32)
    for j in range(CHUNKS):
        end = strided(states_ref, modes * CHUNKS, width, j, modes, CHUNKS)
        for t in range(width // LANES):
            where = pl.ds(t * modes * CHUNKS + j, modes, stride=CHUNKS)
            states_ref[where, :] = state[:, t * LANES : (t + 1) * LANES]
        state = state * over_chunk + end
    decay = jnp.exp(-lam)
    for t in range(width // LANES):
        part = [spread(decay, r, t) for r in range(modes)]
        scale = [spread(coef, r, t) for r in range(modes)]
        begin = tuple(
            states_ref[pl.ds((t * modes + r) * CHUNKS, CHUNKS), :] for r in range(modes)
        )

        def visit(i, carry, t=t, scale=scale):
            total = functools.reduce(jnp.add, [s * h for s, h in zip(scale, carry)])
            conv_ref[pl.ds(t * rows + i, CHUNKS, stride=steps), :] = total

        recur(product_ref, t * rows, part, begin, steps, visit)
    query_ref[...] = query
    base_ref[...] = query * (whole(conv_ref, rows, width) + skip_ref[...] * product)


def carry_kernel(
    recv_ref, query_ref, base_ref, taps_ref, rates_ref, residues_ref, skip_ref, out_ref,
    rims_ref, firsts_ref, states_ref, conv_ref,
):
    blocks = recv_ref.shape[0]
    rows, width = query_ref.shape
    modes = rates_ref.shape[0]
    steps = rows // CHUNKS
    own = lax.axis_index("ctx")
    lam = per_channel(rates_ref[...], width)
    coef = per_channel(residues_ref[...] * jnp.sqrt(2.0 * rates_ref[...]), width)
    skip = skip_ref[...]

    for e in range(blocks):
        edges = recv_ref[e, pl.ds(modes, RIM), :].astype(jnp.float32)
        for t in range(width // LANES):
            rims_ref[pl.ds((t * blocks + e) * RIM, RIM), :] = edges[:, t * LANES : (t + 1) * LANES]

    def edge(k):
        return strided(rims_ref, blocks * RIM, width, k, blocks, RIM)

    block_row = lax.broadcasted_iota(jnp.int32, (blocks, width), 0)

    def earlier(k):
        return jnp.where(block_row == 0, 0.0, pltpu.roll(edge(k), 1, 0))

    def firsts(j, head, tail):
        zeroth, first = edge(head), edge(head + 1)
        before_last, last = earlier(tail), earlier(tail + 1)
        a, b, c = channel_taps(taps_ref, j)
        return a * zeroth + b * last + c * before_last, a * first + b * zeroth + c * last

    query0, query1 = firsts(0, 10, 8)
    key0, key1 = firsts(1, 0, 4)
    value0, value1 = firsts(2, 2, 6)
    product0, product1 = key0 * value0, key1 * value1
    for k, array in enumerate((query0, query1, product0, product1)):
        firsts_ref[pl.ds(k * blocks, blocks), :] = array
    own_query0, own_query1, own_product0, own_product1 = (
        firsts_ref[pl.ds(k * blocks + own, 1), :] for k in range(4)
    )

    over_block = jnp.exp(-lam * float(rows))
    weight0 = jnp.exp(-lam * float(rows - 1))
    weight1 = jnp.exp(-lam * float(rows - 2))
    state = jnp.zeros((modes, width), jnp.float32)
    for e in range(blocks - 1):
        added = (
            recv_ref[e, pl.ds(0, modes), :].astype(jnp.float32)
            + weight0 * product0[e : e + 1]
            + weight1 * product1[e : e + 1]
        )
        state = jnp.where(e < own, state * over_block + added, state)

    decay = jnp.exp(-lam)
    state0 = decay * state + own_product0
    state1 = decay * state0 + own_product1
    gated0, gated1 = (
        q * (jnp.sum(coef * h, 0, keepdims=True) + skip * p)
        for q, h, p in (
            (own_query0, state0, own_product0), (own_query1, state1, own_product1)
        )
    )

    grow = jnp.exp(lam)
    start = coef * (state + grow * (own_product0 + grow * own_product1))
    for j in range(CHUNKS):
        scaled = start * jnp.exp(-lam * float(steps * j))
        for t in range(width // LANES):
            where = pl.ds(t * modes * CHUNKS + j, modes, stride=CHUNKS)
            states_ref[where, :] = scaled[:, t * LANES : (t + 1) * LANES]
    for t in range(width // LANES):
        part = [spread(decay, r, t) for r in range(modes)]
        begin = tuple(
            states_ref[pl.ds((t * modes + r) * CHUNKS, CHUNKS), :] for r in range(modes)
        )

        def step(i, carry, t=t, part=part):
            carry = tuple(d * h for d, h in zip(part, carry))
            where = pl.ds(t * rows + i, CHUNKS, stride=steps)
            conv_ref[where, :] = functools.reduce(jnp.add, carry)
            return carry

        lax.fori_loop(0, steps, step, begin, unroll=4)
    gated = base_ref[...] + query_ref[...] * whole(conv_ref, rows, width)
    row = lax.broadcasted_iota(jnp.int32, (rows, width), 0)
    gated = jnp.where(row == 0, gated0, jnp.where(row == 1, gated1, gated))
    gated = gated.astype(jnp.bfloat16).astype(jnp.float32)
    root = jnp.sqrt(jnp.sqrt(jnp.abs(gated) * 2.0**32))
    out_ref[...] = jnp.where(gated < 0.0, -root, root)


def shards(features, short_taps, residues, rates, skip, out_weight):
    blocks = lax.axis_size("ctx")
    rows, _, width = features.shape
    modes = rates.shape[0]
    feats = features.transpose(1, 0, 2)
    skip = skip.reshape(1, width)
    f32 = jnp.float32
    tiles = width // LANES
    plane = jax.ShapeDtypeStruct((rows, width), f32)
    by_row = pltpu.VMEM((tiles * rows, LANES), f32)
    by_mode = pltpu.VMEM((tiles * modes * CHUNKS, LANES), f32)
    sent = pl.pallas_call(
        state_kernel,
        out_shape=jax.ShapeDtypeStruct((blocks, modes + RIM, width), jnp.bfloat16),
        scratch_shapes=[by_row, by_mode],
        name="block_state",
    )(feats, short_taps, rates)
    received = lax.all_to_all(sent, "ctx", split_axis=0, concat_axis=0, tiled=True)
    query, base = pl.pallas_call(
        local_kernel,
        out_shape=(plane, plane),
        scratch_shapes=[by_row, by_mode, by_row],
        name="local_conv",
    )(feats, short_taps, rates, residues, skip)
    coded = pl.pallas_call(
        carry_kernel,
        out_shape=plane,
        scratch_shapes=[
            pltpu.VMEM((tiles * blocks * RIM, LANES), f32),
            pltpu.VMEM((4 * blocks, width), f32),
            by_mode,
            by_row,
        ],
        name="carry_gate",
    )(received, query, base, short_taps, rates, residues, skip)
    gathered = lax.all_gather(coded.astype(jnp.float16), "tp", axis=1, tiled=True).astype(f32)
    square = gathered * gathered
    gated = (square * (gathered * jnp.abs(gathered)) * 2.0**-32).astype(jnp.bfloat16)
    return jnp.dot(gated, out_weight, preferred_element_type=f32).astype(jnp.bfloat16)


def solution(mesh):
    in_specs = (
        P("ctx", None, "tp"),
        P(None, None, "tp"),
        P(None, "tp"),
        P(None, "tp"),
        P("tp"),
        P(None, "tp"),
    )
    return jax.shard_map(
        shards, mesh=mesh, in_specs=in_specs, out_specs=P("ctx", "tp"), check_vma=False
    )
```

```python
import functools

import jax
import jax.numpy as jnp
from jax import lax
from jax.experimental import pallas as pl
from jax.experimental.pallas import tpu as pltpu
from jax.sharding import PartitionSpec as P

SHORT = 3
CHUNKS = 8
RIM = 16
LANES = 128
TABLES = 7
KERNEL_VMEM = 12 * 2**20
HIGHEST = lax.Precision.HIGHEST


def per_channel(table, width):
    filters = table.shape[1]
    group = width // filters
    row = lax.broadcasted_iota(jnp.int32, (filters, width), 0)
    col = lax.broadcasted_iota(jnp.int32, (filters, width), 1)
    pick = jnp.where(col // group == row, 1.0, 0.0).astype(jnp.float32)
    return lax.dot_general(
        table, pick, (((1,), (0,)), ((), ())), precision=HIGHEST,
        preferred_element_type=jnp.float32,
    )


def short_filter(block, taps, before_last, last):
    row = lax.broadcasted_iota(jnp.int32, block.shape, 0)
    one = jnp.where(row == 0, last, pltpu.roll(block, 1, 0))
    two = jnp.where(row == 0, before_last, jnp.where(row == 1, last, pltpu.roll(block, 2, 0)))
    return taps[0] * block + taps[1] * one + taps[2] * two


def save(ref, array):
    rows, width = array.shape
    for t in range(width // LANES):
        ref[pl.ds(t * rows, rows), :] = array[:, t * LANES : (t + 1) * LANES]


def strided(ref, rows, width, start, count, stride):
    return jnp.concatenate(
        [ref[pl.ds(t * rows + start, count, stride=stride), :] for t in range(width // LANES)], 1
    )


def whole(ref, rows, width):
    return jnp.concatenate([ref[pl.ds(t * rows, rows), :] for t in range(width // LANES)], 1)


def spread(table, r, t):
    return jnp.broadcast_to(table[r : r + 1, t * LANES : (t + 1) * LANES], (CHUNKS, LANES))


def recur(product_ref, base, decay, states, steps, visit=None):
    def step(i, carry):
        now = product_ref[pl.ds(base + i, CHUNKS, stride=steps), :]
        carry = tuple(d * h + now for d, h in zip(decay, carry))
        if visit is not None:
            visit(i, carry)
        return carry

    return lax.fori_loop(0, steps, step, states, unroll=4)


def chunk_ends(product_ref, ends_ref, lam, rows):
    modes, width = lam.shape
    decay = jnp.exp(-lam)
    for t in range(width // LANES):
        blank = tuple(jnp.zeros((CHUNKS, LANES), jnp.float32) for _ in range(modes))
        part = [spread(decay, r, t) for r in range(modes)]
        ends = recur(product_ref, t * rows, part, blank, rows // CHUNKS)
        for r, end in enumerate(ends):
            ends_ref[pl.ds((t * modes + r) * CHUNKS, CHUNKS), :] = end


def channel_taps(taps_ref, j):
    return [taps_ref[s, j : j + 1, :] for s in range(SHORT)]


def inner_product(feat_ref, taps_ref):
    rows, width = feat_ref.shape[1:]
    zero = jnp.zeros((1, width), jnp.float32)
    keys, values = (
        short_filter(feat_ref[j].astype(jnp.float32), channel_taps(taps_ref, j), zero, zero)
        for j in (1, 2)
    )
    row = lax.broadcasted_iota(jnp.int32, (rows, width), 0)
    return jnp.where(row < SHORT - 1, 0.0, keys * values)


def state_kernel(
    feat_hbm, taps_hbm, rates_hbm, send_ref,
    feat_ref, taps_ref, rates_ref, product_ref, ends_ref, sems,
):
    copies = [
        pltpu.make_async_copy(source, target, sems.at[k])
        for k, (source, target) in enumerate(
            ((feat_hbm, feat_ref), (taps_hbm, taps_ref), (rates_hbm, rates_ref))
        )
    ]
    for copy in copies:
        copy.start()
    for copy in copies:
        copy.wait()
    rows, width = feat_ref.shape[1:]
    modes = rates_ref.shape[0]
    lam = per_channel(rates_ref[...], width)
    save(product_ref, inner_product(feat_ref, taps_ref))
    chunk_ends(product_ref, ends_ref, lam, rows)
    over_chunk = jnp.exp(-lam * float(rows // CHUNKS))
    total = jnp.zeros((modes, width), jnp.float32)
    for j in range(CHUNKS):
        end = strided(ends_ref, modes * CHUNKS, width, j, modes, CHUNKS)
        total = total * over_chunk + end
    head = [feat_ref[j, 0:2, :].astype(jnp.float32) for j in (1, 2)]
    tail = [feat_ref[j, rows - 2 : rows, :].astype(jnp.float32) for j in (1, 2, 0)]
    own_query = [feat_ref[0, 0:2, :].astype(jnp.float32)]
    blank = [jnp.zeros((RIM - 12, width), jnp.float32)]
    rim = jnp.concatenate(head + tail + own_query + blank, 0)
    block = jnp.concatenate([total, rim], 0).astype(jnp.bfloat16)
    for e in range(send_ref.shape[0]):
        send_ref[e] = block


def local_kernel(
    feat_ref, taps_ref, rates_ref, residues_ref, skip_ref, local_ref,
    product_ref, states_ref, conv_ref,
):
    rows, width = feat_ref.shape[1:]
    modes = rates_ref.shape[0]
    steps = rows // CHUNKS
    lam = per_channel(rates_ref[...], width)
    coef = per_channel(residues_ref[...] * jnp.sqrt(2.0 * rates_ref[...]), width)
    zero = jnp.zeros((1, width), jnp.float32)
    query = short_filter(feat_ref[0].astype(jnp.float32), channel_taps(taps_ref, 0), zero, zero)
    product = inner_product(feat_ref, taps_ref)
    save(product_ref, product)
    chunk_ends(product_ref, states_ref, lam, rows)
    over_chunk = jnp.exp(-lam * float(steps))
    state = jnp.zeros((modes, width), jnp.float32)
    for j in range(CHUNKS):
        end = strided(states_ref, modes * CHUNKS, width, j, modes, CHUNKS)
        for t in range(width // LANES):
            where = pl.ds(t * modes * CHUNKS + j, modes, stride=CHUNKS)
            states_ref[where, :] = state[:, t * LANES : (t + 1) * LANES]
        state = state * over_chunk + end
    decay = jnp.exp(-lam)
    for t in range(width // LANES):
        part = [spread(decay, r, t) for r in range(modes)]
        scale = [spread(coef, r, t) for r in range(modes)]
        begin = tuple(
            states_ref[pl.ds((t * modes + r) * CHUNKS, CHUNKS), :] for r in range(modes)
        )

        def visit(i, carry, t=t, scale=scale):
            total = functools.reduce(jnp.add, [s * h for s, h in zip(scale, carry)])
            conv_ref[pl.ds(t * rows + i, CHUNKS, stride=steps), :] = total

        recur(product_ref, t * rows, part, begin, steps, visit)
    for k, table in enumerate(
        (
            decay,
            jnp.exp(lam),
            jnp.exp(-lam * float(rows - 2)),
            jnp.exp(-lam * float(rows - 1)),
            jnp.exp(-lam * float(rows)),
            over_chunk,
            coef,
        )
    ):
        local_ref[pl.ds(2 * rows + k * modes, modes), :] = table
    singles = 2 * rows + TABLES * modes
    for j in range(3):
        for shift, tap in enumerate(channel_taps(taps_ref, j)):
            local_ref[pl.ds(singles + SHORT * j + shift, 1), :] = tap
    local_ref[pl.ds(singles + 3 * SHORT, 1), :] = skip_ref[...]
    local_ref[pl.ds(0, rows), :] = query
    local_ref[pl.ds(rows, rows), :] = query * (whole(conv_ref, rows, width) + skip_ref[...] * product)


def carry_kernel(
    recv_ref, local_ref, out_ref,
    rims_ref, firsts_ref, states_ref, conv_ref,
):
    blocks = recv_ref.shape[0]
    rows, width = out_ref.shape
    modes = recv_ref.shape[1] - RIM
    steps = rows // CHUNKS
    own = lax.axis_index("ctx")
    decay, grow, weight1, weight0, over_block, over_chunk, coef = (
        local_ref[pl.ds(2 * rows + k * modes, modes), :] for k in range(TABLES)
    )

    def single(k):
        return local_ref[pl.ds(2 * rows + TABLES * modes + k, 1), :]

    skip = single(3 * SHORT)

    for e in range(blocks):
        edges = recv_ref[e, pl.ds(modes, RIM), :].astype(jnp.float32)
        for t in range(width // LANES):
            rims_ref[pl.ds((t * blocks + e) * RIM, RIM), :] = edges[:, t * LANES : (t + 1) * LANES]

    def edge(k):
        return strided(rims_ref, blocks * RIM, width, k, blocks, RIM)

    block_row = lax.broadcasted_iota(jnp.int32, (blocks, width), 0)

    def earlier(k):
        return jnp.where(block_row == 0, 0.0, pltpu.roll(edge(k), 1, 0))

    def firsts(j, head, tail):
        zeroth, first = edge(head), edge(head + 1)
        before_last, last = earlier(tail), earlier(tail + 1)
        a, b, c = (single(SHORT * j + shift) for shift in range(SHORT))
        return a * zeroth + b * last + c * before_last, a * first + b * zeroth + c * last

    query0, query1 = firsts(0, 10, 8)
    key0, key1 = firsts(1, 0, 4)
    value0, value1 = firsts(2, 2, 6)
    product0, product1 = key0 * value0, key1 * value1
    for k, array in enumerate((query0, query1, product0, product1)):
        firsts_ref[pl.ds(k * blocks, blocks), :] = array
    own_query0, own_query1, own_product0, own_product1 = (
        firsts_ref[pl.ds(k * blocks + own, 1), :] for k in range(4)
    )

    state = jnp.zeros((modes, width), jnp.float32)
    for e in range(blocks - 1):
        added = (
            recv_ref[e, pl.ds(0, modes), :].astype(jnp.float32)
            + weight0 * product0[e : e + 1]
            + weight1 * product1[e : e + 1]
        )
        state = jnp.where(e < own, state * over_block + added, state)

    state0 = decay * state + own_product0
    state1 = decay * state0 + own_product1
    gated0, gated1 = (
        q * (jnp.sum(coef * h, 0, keepdims=True) + skip * p)
        for q, h, p in (
            (own_query0, state0, own_product0), (own_query1, state1, own_product1)
        )
    )

    start = coef * (state + grow * (own_product0 + grow * own_product1))
    for j in range(CHUNKS):
        for t in range(width // LANES):
            where = pl.ds(t * modes * CHUNKS + j, modes, stride=CHUNKS)
            states_ref[where, :] = start[:, t * LANES : (t + 1) * LANES]
        start = start * over_chunk
    for t in range(width // LANES):
        part = [spread(decay, r, t) for r in range(modes)]
        begin = tuple(
            states_ref[pl.ds((t * modes + r) * CHUNKS, CHUNKS), :] for r in range(modes)
        )

        def step(i, carry, t=t, part=part):
            carry = tuple(d * h for d, h in zip(part, carry))
            where = pl.ds(t * rows + i, CHUNKS, stride=steps)
            conv_ref[where, :] = functools.reduce(jnp.add, carry)
            return carry

        lax.fori_loop(0, steps, step, begin, unroll=4)
    query, base = local_ref[pl.ds(0, rows), :], local_ref[pl.ds(rows, rows), :]
    gated = base + query * whole(conv_ref, rows, width)
    row = lax.broadcasted_iota(jnp.int32, (rows, width), 0)
    gated = jnp.where(row == 0, gated0, jnp.where(row == 1, gated1, gated))
    gated = gated.astype(jnp.bfloat16).astype(jnp.float32)
    root = jnp.sqrt(jnp.sqrt(jnp.abs(gated) * 2.0**32))
    out_ref[...] = jnp.where(gated < 0.0, -root, root)


def shards(features, short_taps, residues, rates, skip, out_weight):
    blocks = lax.axis_size("ctx")
    rows, _, width = features.shape
    modes = rates.shape[0]
    feats = features.transpose(1, 0, 2)
    skip = skip.reshape(1, width)
    f32 = jnp.float32
    tiles = width // LANES
    plane = jax.ShapeDtypeStruct((rows, width), f32)
    by_row = pltpu.VMEM((tiles * rows, LANES), f32)
    by_mode = pltpu.VMEM((tiles * modes * CHUNKS, LANES), f32)
    whole_in = pl.BlockSpec(memory_space=pltpu.VMEM)
    sent = pl.pallas_call(
        state_kernel,
        in_specs=[pl.BlockSpec(memory_space=pltpu.HBM)] * 3,
        out_specs=whole_in,
        out_shape=jax.ShapeDtypeStruct((blocks, modes + RIM, width), jnp.bfloat16),
        scratch_shapes=[
            pltpu.VMEM(feats.shape, feats.dtype),
            pltpu.VMEM(short_taps.shape, f32),
            pltpu.VMEM(rates.shape, f32),
            by_row,
            by_mode,
            pltpu.SemaphoreType.DMA((3,)),
        ],
        name="block_state",
    )(feats, short_taps, rates)
    received = lax.all_to_all(sent, "ctx", split_axis=0, concat_axis=0, tiled=True)
    local = pl.pallas_call(
        local_kernel,
        in_specs=[whole_in] * 5,
        out_specs=whole_in,
        out_shape=jax.ShapeDtypeStruct((2 * rows + (TABLES + 1) * modes, width), f32),
        scratch_shapes=[by_row, by_mode, by_row],
        compiler_params=pltpu.CompilerParams(vmem_limit_bytes=KERNEL_VMEM),
        name="local_conv",
    )(feats, short_taps, rates, residues, skip)
    coded = pl.pallas_call(
        carry_kernel,
        in_specs=[whole_in] * 2,
        out_specs=whole_in,
        out_shape=plane,
        scratch_shapes=[
            pltpu.VMEM((tiles * blocks * RIM, LANES), f32),
            pltpu.VMEM((4 * blocks, width), f32),
            by_mode,
            by_row,
        ],
        compiler_params=pltpu.CompilerParams(vmem_limit_bytes=KERNEL_VMEM),
        name="carry_gate",
    )(received, local)
    gathered = lax.all_gather(coded.astype(jnp.float16), "tp", axis=1, tiled=True).astype(f32)
    square = gathered * gathered
    gated = (square * (gathered * jnp.abs(gathered)) * 2.0**-32).astype(jnp.bfloat16)
    return jnp.dot(gated, out_weight, preferred_element_type=f32).astype(jnp.bfloat16)


def solution(mesh):
    in_specs = (
        P("ctx", None, "tp"),
        P(None, None, "tp"),
        P(None, "tp"),
        P(None, "tp"),
        P("tp"),
        P(None, "tp"),
    )
    return jax.shard_map(
        shards, mesh=mesh, in_specs=in_specs, out_specs=P("ctx", "tp"), check_vma=False
    )
```

```python
import functools

import jax
import jax.numpy as jnp
from jax import lax
from jax.experimental import pallas as pl
from jax.experimental.pallas import tpu as pltpu
from jax.sharding import PartitionSpec as P

SHORT = 3
CHUNKS = 8
RIM = 8
EDGE = 16
LANES = 128
TABLES = 7
KERNEL_VMEM = 12 * 2**20
HIGHEST = lax.Precision.HIGHEST


def per_channel(table, width):
    filters = table.shape[1]
    group = width // filters
    row = lax.broadcasted_iota(jnp.int32, (filters, width), 0)
    col = lax.broadcasted_iota(jnp.int32, (filters, width), 1)
    pick = jnp.where(col // group == row, 1.0, 0.0).astype(jnp.float32)
    return lax.dot_general(
        table, pick, (((1,), (0,)), ((), ())), precision=HIGHEST,
        preferred_element_type=jnp.float32,
    )


def short_filter(block, taps, before_last, last):
    row = lax.broadcasted_iota(jnp.int32, block.shape, 0)
    one = jnp.where(row == 0, last, pltpu.roll(block, 1, 0))
    two = jnp.where(row == 0, before_last, jnp.where(row == 1, last, pltpu.roll(block, 2, 0)))
    return taps[0] * block + taps[1] * one + taps[2] * two


def save(ref, array):
    rows, width = array.shape
    for t in range(width // LANES):
        ref[pl.ds(t * rows, rows), :] = array[:, t * LANES : (t + 1) * LANES]


def strided(ref, rows, width, start, count, stride):
    return jnp.concatenate(
        [ref[pl.ds(t * rows + start, count, stride=stride), :] for t in range(width // LANES)], 1
    )


def whole(ref, rows, width):
    return jnp.concatenate([ref[pl.ds(t * rows, rows), :] for t in range(width // LANES)], 1)


def spread(table, r, t):
    return jnp.broadcast_to(table[r : r + 1, t * LANES : (t + 1) * LANES], (CHUNKS, LANES))


def recur(product_ref, base, decay, states, steps, visit=None):
    def step(i, carry):
        now = product_ref[pl.ds(base + i, CHUNKS, stride=steps), :]
        carry = tuple(d * h + now for d, h in zip(decay, carry))
        if visit is not None:
            visit(i, carry)
        return carry

    return lax.fori_loop(0, steps, step, states, unroll=8)


def chunk_ends(product_ref, ends_ref, lam, rows):
    modes, width = lam.shape
    decay = jnp.exp(-lam)
    for t in range(width // LANES):
        blank = tuple(jnp.zeros((CHUNKS, LANES), jnp.float32) for _ in range(modes))
        part = [spread(decay, r, t) for r in range(modes)]
        ends = recur(product_ref, t * rows, part, blank, rows // CHUNKS)
        for r, end in enumerate(ends):
            ends_ref[pl.ds((t * modes + r) * CHUNKS, CHUNKS), :] = end


def channel_taps(taps_ref, j):
    return [taps_ref[s, j : j + 1, :] for s in range(SHORT)]


def inner_product(feat_ref, taps_ref):
    rows, width = feat_ref.shape[1:]
    zero = jnp.zeros((1, width), jnp.float32)
    keys, values = (
        short_filter(feat_ref[j].astype(jnp.float32), channel_taps(taps_ref, j), zero, zero)
        for j in (1, 2)
    )
    row = lax.broadcasted_iota(jnp.int32, (rows, width), 0)
    return jnp.where(row < SHORT - 1, 0.0, keys * values)


def state_kernel(
    feat_hbm, taps_hbm, rates_hbm, send_ref, edge_ref,
    feat_ref, taps_ref, rates_ref, product_ref, ends_ref, sems,
):
    copies = [
        pltpu.make_async_copy(source, target, sems.at[k])
        for k, (source, target) in enumerate(
            ((rates_hbm, rates_ref), (taps_hbm, taps_ref), (feat_hbm, feat_ref))
        )
    ]
    for copy in copies:
        copy.start()
    rows, width = feat_ref.shape[1:]
    modes = rates_ref.shape[0]
    copies[0].wait()
    lam = per_channel(rates_ref[...], width)
    copies[1].wait()
    copies[2].wait()
    save(product_ref, inner_product(feat_ref, taps_ref))
    chunk_ends(product_ref, ends_ref, lam, rows)
    over_chunk = jnp.exp(-lam * float(rows // CHUNKS))
    total = jnp.zeros((modes, width), jnp.float32)
    for j in range(CHUNKS):
        end = strided(ends_ref, modes * CHUNKS, width, j, modes, CHUNKS)
        total = total * over_chunk + end
    edges = [
        feat_ref[j, pl.ds(first, EDGE), :].astype(jnp.float32)[at : at + 2]
        for first, at in ((0, 0), (rows - EDGE, EDGE - 2))
        for j in (1, 2)
    ]
    block = jnp.concatenate([total] + edges, 0).astype(jnp.bfloat16)
    edge_ref[...] = feat_ref[0, pl.ds(rows - EDGE, EDGE), :]
    for e in range(send_ref.shape[0]):
        send_ref[e] = block


def local_kernel(
    feat_ref, taps_ref, rates_ref, residues_ref, skip_ref, local_ref,
    product_ref, states_ref, conv_ref,
):
    rows, width = feat_ref.shape[1:]
    modes = rates_ref.shape[0]
    steps = rows // CHUNKS
    lam = per_channel(rates_ref[...], width)
    coef = per_channel(residues_ref[...] * jnp.sqrt(2.0 * rates_ref[...]), width)
    zero = jnp.zeros((1, width), jnp.float32)
    query = short_filter(feat_ref[0].astype(jnp.float32), channel_taps(taps_ref, 0), zero, zero)
    product = inner_product(feat_ref, taps_ref)
    save(product_ref, product)
    chunk_ends(product_ref, states_ref, lam, rows)
    over_chunk = jnp.exp(-lam * float(steps))
    state = jnp.zeros((modes, width), jnp.float32)
    for j in range(CHUNKS):
        end = strided(states_ref, modes * CHUNKS, width, j, modes, CHUNKS)
        for t in range(width // LANES):
            where = pl.ds(t * modes * CHUNKS + j, modes, stride=CHUNKS)
            states_ref[where, :] = state[:, t * LANES : (t + 1) * LANES]
        state = state * over_chunk + end
    decay = jnp.exp(-lam)
    for t in range(width // LANES):
        part = [spread(decay, r, t) for r in range(modes)]
        scale = [spread(coef, r, t) for r in range(modes)]
        begin = tuple(
            states_ref[pl.ds((t * modes + r) * CHUNKS, CHUNKS), :] for r in range(modes)
        )

        def visit(i, carry, t=t, scale=scale):
            total = functools.reduce(jnp.add, [s * h for s, h in zip(scale, carry)])
            conv_ref[pl.ds(t * rows + i, CHUNKS, stride=steps), :] = total

        recur(product_ref, t * rows, part, begin, steps, visit)
    for k, table in enumerate(
        (
            decay,
            jnp.exp(lam),
            jnp.exp(-lam * float(rows - 2)),
            jnp.exp(-lam * float(rows - 1)),
            jnp.exp(-lam * float(rows)),
            over_chunk,
            coef,
        )
    ):
        local_ref[pl.ds(2 * rows + k * modes, modes), :] = table
    singles = 2 * rows + TABLES * modes
    for j in range(3):
        for shift, tap in enumerate(channel_taps(taps_ref, j)):
            local_ref[pl.ds(singles + SHORT * j + shift, 1), :] = tap
    local_ref[pl.ds(singles + 3 * SHORT, 1), :] = skip_ref[...]
    local_ref[pl.ds(0, rows), :] = query
    local_ref[pl.ds(rows, rows), :] = query * (whole(conv_ref, rows, width) + skip_ref[...] * product)


def carry_kernel(
    recv_ref, edge_ref, local_ref, out_ref,
    rims_ref, firsts_ref, states_ref, conv_ref,
):
    blocks = recv_ref.shape[0]
    rows, width = out_ref.shape
    modes = recv_ref.shape[1] - RIM
    steps = rows // CHUNKS
    own = lax.axis_index("ctx")
    decay, grow, weight1, weight0, over_block, over_chunk, coef = (
        local_ref[pl.ds(2 * rows + k * modes, modes), :] for k in range(TABLES)
    )

    def single(k):
        return local_ref[pl.ds(2 * rows + TABLES * modes + k, 1), :]

    skip = single(3 * SHORT)

    for e in range(blocks):
        edges = recv_ref[e].astype(jnp.float32)[modes : modes + RIM]
        for t in range(width // LANES):
            rims_ref[pl.ds((t * blocks + e) * RIM, RIM), :] = edges[:, t * LANES : (t + 1) * LANES]

    def edge(k):
        return strided(rims_ref, blocks * RIM, width, k, blocks, RIM)

    block_row = lax.broadcasted_iota(jnp.int32, (blocks, width), 0)

    def earlier(k):
        return jnp.where(block_row == 0, 0.0, pltpu.roll(edge(k), 1, 0))

    def firsts(j, head, tail):
        zeroth, first = edge(head), edge(head + 1)
        before_last, last = earlier(tail), earlier(tail + 1)
        a, b, c = (single(SHORT * j + shift) for shift in range(SHORT))
        return a * zeroth + b * last + c * before_last, a * first + b * zeroth + c * last

    key0, key1 = firsts(1, 0, 4)
    value0, value1 = firsts(2, 2, 6)
    product0, product1 = key0 * value0, key1 * value1
    for k, array in enumerate((product0, product1)):
        firsts_ref[pl.ds(k * blocks, blocks), :] = array
    own_product0, own_product1 = (firsts_ref[pl.ds(k * blocks + own, 1), :] for k in range(2))
    before = edge_ref[...].astype(jnp.float32)
    before_last, last = before[EDGE - 2 : EDGE - 1], before[EDGE - 1 : EDGE]
    own_query0 = local_ref[pl.ds(0, 1), :] + single(1) * last + single(2) * before_last
    own_query1 = local_ref[pl.ds(1, 1), :] + single(2) * last

    state = jnp.zeros((modes, width), jnp.float32)
    for e in range(blocks - 1):
        added = (
            recv_ref[e, pl.ds(0, modes), :].astype(jnp.float32)
            + weight0 * product0[e : e + 1]
            + weight1 * product1[e : e + 1]
        )
        state = jnp.where(e < own, state * over_block + added, state)

    state0 = decay * state + own_product0
    state1 = decay * state0 + own_product1
    gated0, gated1 = (
        q * (jnp.sum(coef * h, 0, keepdims=True) + skip * p)
        for q, h, p in (
            (own_query0, state0, own_product0), (own_query1, state1, own_product1)
        )
    )

    start = coef * (state + grow * (own_product0 + grow * own_product1))
    for j in range(CHUNKS):
        for t in range(width // LANES):
            where = pl.ds(t * modes * CHUNKS + j, modes, stride=CHUNKS)
            states_ref[where, :] = start[:, t * LANES : (t + 1) * LANES]
        start = start * over_chunk
    for t in range(width // LANES):
        part = [spread(decay, r, t) for r in range(modes)]
        begin = tuple(
            states_ref[pl.ds((t * modes + r) * CHUNKS, CHUNKS), :] for r in range(modes)
        )

        def step(i, carry, t=t, part=part):
            carry = tuple(d * h for d, h in zip(part, carry))
            where = pl.ds(t * rows + i, CHUNKS, stride=steps)
            conv_ref[where, :] = functools.reduce(jnp.add, carry)
            return carry

        lax.fori_loop(0, steps, step, begin, unroll=4)
    query, base = local_ref[pl.ds(0, rows), :], local_ref[pl.ds(rows, rows), :]
    gated = base + query * whole(conv_ref, rows, width)
    row = lax.broadcasted_iota(jnp.int32, (rows, width), 0)
    gated = jnp.where(row == 0, gated0, jnp.where(row == 1, gated1, gated))
    gated = gated.astype(jnp.bfloat16).astype(jnp.float32)
    root = jnp.sqrt(jnp.sqrt(jnp.abs(gated) * 2.0**32))
    out_ref[...] = jnp.where(gated < 0.0, -root, root)


def shards(features, short_taps, residues, rates, skip, out_weight):
    blocks = lax.axis_size("ctx")
    rows, _, width = features.shape
    modes = rates.shape[0]
    feats = features.transpose(1, 0, 2)
    skip = skip.reshape(1, width)
    f32 = jnp.float32
    tiles = width // LANES
    plane = jax.ShapeDtypeStruct((rows, width), f32)
    by_row = pltpu.VMEM((tiles * rows, LANES), f32)
    by_mode = pltpu.VMEM((tiles * modes * CHUNKS, LANES), f32)
    whole_in = pl.BlockSpec(memory_space=pltpu.VMEM)
    sent, edge = pl.pallas_call(
        state_kernel,
        in_specs=[pl.BlockSpec(memory_space=pltpu.HBM)] * 3,
        out_specs=(whole_in, whole_in),
        out_shape=(
            jax.ShapeDtypeStruct((blocks, modes + RIM, width), jnp.bfloat16),
            jax.ShapeDtypeStruct((EDGE, width), jnp.bfloat16),
        ),
        scratch_shapes=[
            pltpu.VMEM(feats.shape, feats.dtype),
            pltpu.VMEM(short_taps.shape, f32),
            pltpu.VMEM(rates.shape, f32),
            by_row,
            by_mode,
            pltpu.SemaphoreType.DMA((3,)),
        ],
        name="block_state",
    )(feats, short_taps, rates)
    received = lax.all_to_all(sent, "ctx", split_axis=0, concat_axis=0, tiled=True)
    before = lax.ppermute(edge, "ctx", [(i, i + 1) for i in range(blocks - 1)])
    local = pl.pallas_call(
        local_kernel,
        in_specs=[whole_in] * 5,
        out_specs=whole_in,
        out_shape=jax.ShapeDtypeStruct((2 * rows + (TABLES + 1) * modes, width), f32),
        scratch_shapes=[by_row, by_mode, by_row],
        compiler_params=pltpu.CompilerParams(vmem_limit_bytes=KERNEL_VMEM),
        name="local_conv",
    )(feats, short_taps, rates, residues, skip)
    coded = pl.pallas_call(
        carry_kernel,
        in_specs=[whole_in] * 3,
        out_specs=whole_in,
        out_shape=plane,
        scratch_shapes=[
            pltpu.VMEM((tiles * blocks * RIM, LANES), f32),
            pltpu.VMEM((2 * blocks, width), f32),
            by_mode,
            by_row,
        ],
        compiler_params=pltpu.CompilerParams(vmem_limit_bytes=KERNEL_VMEM),
        name="carry_gate",
    )(received, before, local)
    gathered = lax.all_gather(coded.astype(jnp.float16), "tp", axis=1, tiled=True).astype(f32)
    square = gathered * gathered
    gated = (square * (gathered * jnp.abs(gathered))).astype(jnp.bfloat16)
    mixed = jnp.dot(gated, out_weight, preferred_element_type=f32)
    return (mixed * 2.0**-32).astype(jnp.bfloat16)


def solution(mesh):
    in_specs = (
        P("ctx", None, "tp"),
        P(None, None, "tp"),
        P(None, "tp"),
        P(None, "tp"),
        P("tp"),
        P(None, "tp"),
    )
    return jax.shard_map(
        shards, mesh=mesh, in_specs=in_specs, out_specs=P("ctx", "tp"), check_vma=False
    )
```

```python
import functools

import jax
import jax.numpy as jnp
from jax import lax
from jax.experimental import pallas as pl
from jax.experimental.pallas import tpu as pltpu
from jax.sharding import PartitionSpec as P

SHORT = 3
CHUNKS = 8
RIM = 8
EDGE = 16
LANES = 128
TABLES = 7
KERNEL_VMEM = 12 * 2**20
HIGHEST = lax.Precision.HIGHEST


def per_channel(table, width):
    filters = table.shape[1]
    group = width // filters
    row = lax.broadcasted_iota(jnp.int32, (filters, width), 0)
    col = lax.broadcasted_iota(jnp.int32, (filters, width), 1)
    pick = jnp.where(col // group == row, 1.0, 0.0).astype(jnp.float32)
    return lax.dot_general(
        table, pick, (((1,), (0,)), ((), ())), precision=HIGHEST,
        preferred_element_type=jnp.float32,
    )


def short_filter(block, taps, before_last, last):
    row = lax.broadcasted_iota(jnp.int32, block.shape, 0)
    one = jnp.where(row == 0, last, pltpu.roll(block, 1, 0))
    two = jnp.where(row == 0, before_last, jnp.where(row == 1, last, pltpu.roll(block, 2, 0)))
    return taps[0] * block + taps[1] * one + taps[2] * two


def save(ref, array):
    rows, width = array.shape
    for t in range(width // LANES):
        ref[pl.ds(t * rows, rows), :] = array[:, t * LANES : (t + 1) * LANES]


def strided(ref, rows, width, start, count, stride):
    return jnp.concatenate(
        [ref[pl.ds(t * rows + start, count, stride=stride), :] for t in range(width // LANES)], 1
    )


def whole(ref, rows, width):
    return jnp.concatenate([ref[pl.ds(t * rows, rows), :] for t in range(width // LANES)], 1)


def spread(table, r, t):
    return jnp.broadcast_to(table[r : r + 1, t * LANES : (t + 1) * LANES], (CHUNKS, LANES))


def recur(product_ref, base, decay, states, steps, visit=None):
    def step(i, carry):
        now = product_ref[pl.ds(base + i, CHUNKS, stride=steps), :]
        carry = tuple(d * h + now for d, h in zip(decay, carry))
        if visit is not None:
            visit(i, carry)
        return carry

    return lax.fori_loop(0, steps, step, states, unroll=16)


def chunk_ends(product_ref, ends_ref, decay, rows):
    modes, width = decay.shape
    for t in range(width // LANES):
        blank = tuple(jnp.zeros((CHUNKS, LANES), jnp.float32) for _ in range(modes))
        part = [spread(decay, r, t) for r in range(modes)]
        ends = recur(product_ref, t * rows, part, blank, rows // CHUNKS)
        for r, end in enumerate(ends):
            ends_ref[pl.ds((t * modes + r) * CHUNKS, CHUNKS), :] = end


def table(tables_ref, modes, k):
    return tables_ref[pl.ds(k * modes, modes), :]


def single(tables_ref, modes, k):
    return tables_ref[pl.ds(TABLES * modes + k, 1), :]


def channel_taps(tables_ref, modes, j):
    return [single(tables_ref, modes, SHORT * j + shift) for shift in range(SHORT)]


def inner_product(feat_ref, tables_ref, modes):
    rows, width = feat_ref.shape[1:]
    zero = jnp.zeros((1, width), jnp.float32)
    keys, values = (
        short_filter(
            feat_ref[j].astype(jnp.float32), channel_taps(tables_ref, modes, j), zero, zero
        )
        for j in (1, 2)
    )
    row = lax.broadcasted_iota(jnp.int32, (rows, width), 0)
    return jnp.where(row < SHORT - 1, 0.0, keys * values)


def state_kernel(
    feat_hbm, taps_hbm, rates_hbm, residues_hbm, skip_hbm, send_ref, edge_ref, tables_ref,
    feat_ref, taps_ref, rates_ref, residues_ref, skip_ref, product_ref, ends_ref, sems,
):
    copies = [
        pltpu.make_async_copy(source, target, sems.at[k])
        for k, (source, target) in enumerate(
            (
                (rates_hbm, rates_ref), (residues_hbm, residues_ref), (taps_hbm, taps_ref),
                (skip_hbm, skip_ref), (feat_hbm, feat_ref),
            )
        )
    ]
    for copy in copies:
        copy.start()
    rows, width = feat_ref.shape[1:]
    modes = rates_ref.shape[0]
    steps = rows // CHUNKS
    copies[0].wait()
    copies[1].wait()
    rates = rates_ref[...]
    lam = per_channel(rates, width)
    decay = jnp.exp(-lam)
    over_chunk = jnp.exp(-lam * float(steps))
    coef = per_channel(residues_ref[...] * jnp.sqrt(2.0 * rates), width)
    for k, values in enumerate(
        (
            decay,
            jnp.exp(lam),
            jnp.exp(-lam * float(rows - 2)),
            jnp.exp(-lam * float(rows - 1)),
            jnp.exp(-lam * float(rows)),
            over_chunk,
            coef,
        )
    ):
        tables_ref[pl.ds(k * modes, modes), :] = values
    copies[2].wait()
    copies[3].wait()
    taps = [taps_ref[shift, j : j + 1, :] for j in range(3) for shift in range(SHORT)]
    unused = [jnp.zeros((modes - 3 * SHORT - 1, width), jnp.float32)]
    tables_ref[pl.ds(TABLES * modes, modes), :] = jnp.concatenate(
        taps + [skip_ref[...]] + unused, 0
    )
    copies[4].wait()
    save(product_ref, inner_product(feat_ref, tables_ref, modes))
    chunk_ends(product_ref, ends_ref, decay, rows)
    total = jnp.zeros((modes, width), jnp.float32)
    for j in range(CHUNKS):
        end = strided(ends_ref, modes * CHUNKS, width, j, modes, CHUNKS)
        total = total * over_chunk + end
    edges = [
        feat_ref[j, pl.ds(first, EDGE), :].astype(jnp.float32)[at : at + 2]
        for first, at in ((0, 0), (rows - EDGE, EDGE - 2))
        for j in (1, 2)
    ]
    edges = jnp.concatenate(edges, 0)
    block = jnp.concatenate(
        [a[:, t * LANES : (t + 1) * LANES] for a in (total, edges) for t in range(width // LANES)], 0
    )
    block = block.astype(jnp.bfloat16)
    edge_ref[...] = feat_ref[0, pl.ds(rows - EDGE, EDGE), :]
    for e in range(send_ref.shape[0]):
        send_ref[e] = block


def local_kernel(feat_ref, tables_ref, local_ref, product_ref, states_ref, conv_ref):
    rows, width = feat_ref.shape[1:]
    modes = tables_ref.shape[0] // (TABLES + 1)
    steps = rows // CHUNKS
    decay, over_chunk, coef = (table(tables_ref, modes, k) for k in (0, 5, 6))
    zero = jnp.zeros((1, width), jnp.float32)
    query = short_filter(
        feat_ref[0].astype(jnp.float32), channel_taps(tables_ref, modes, 0), zero, zero
    )
    product = inner_product(feat_ref, tables_ref, modes)
    save(product_ref, product)
    chunk_ends(product_ref, states_ref, decay, rows)
    state = jnp.zeros((modes, width), jnp.float32)
    for j in range(CHUNKS):
        end = strided(states_ref, modes * CHUNKS, width, j, modes, CHUNKS)
        for t in range(width // LANES):
            where = pl.ds(t * modes * CHUNKS + j, modes, stride=CHUNKS)
            states_ref[where, :] = state[:, t * LANES : (t + 1) * LANES]
        state = state * over_chunk + end
    for t in range(width // LANES):
        part = [spread(decay, r, t) for r in range(modes)]
        scale = [spread(coef, r, t) for r in range(modes)]
        begin = tuple(
            states_ref[pl.ds((t * modes + r) * CHUNKS, CHUNKS), :] for r in range(modes)
        )

        def visit(i, carry, t=t, scale=scale):
            total = functools.reduce(jnp.add, [s * h for s, h in zip(scale, carry)])
            conv_ref[pl.ds(t * rows + i, CHUNKS, stride=steps), :] = total

        recur(product_ref, t * rows, part, begin, steps, visit)
    skip = single(tables_ref, modes, 3 * SHORT)
    local_ref[pl.ds(2 * rows, (TABLES + 1) * modes), :] = tables_ref[...]
    local_ref[pl.ds(0, rows), :] = query
    local_ref[pl.ds(rows, rows), :] = query * (whole(conv_ref, rows, width) + skip * product)


def carry_kernel(
    recv_ref, edge_ref, local_ref, out_ref,
    rims_ref, firsts_ref, states_ref, conv_ref,
):
    blocks = recv_ref.shape[0]
    rows, width = out_ref.shape
    tiles = width // LANES
    modes = recv_ref.shape[1] // tiles - RIM
    steps = rows // CHUNKS
    own = lax.axis_index("ctx")
    tables_ref = local_ref.at[pl.ds(2 * rows, (TABLES + 1) * modes)]
    decay, grow, weight1, weight0, over_block, over_chunk, coef = (
        table(tables_ref, modes, k) for k in range(TABLES)
    )
    skip = single(tables_ref, modes, 3 * SHORT)

    for e in range(blocks):
        edges = recv_ref[e, pl.ds(tiles * modes, tiles * RIM), :].astype(jnp.float32)
        rims_ref[pl.ds(e * tiles * RIM, tiles * RIM), :] = edges

    def edge(k):
        return strided(rims_ref, RIM, width, k, blocks, tiles * RIM)

    block_row = lax.broadcasted_iota(jnp.int32, (blocks, width), 0)

    def earlier(k):
        return jnp.where(block_row == 0, 0.0, pltpu.roll(edge(k), 1, 0))

    def firsts(j, head, tail):
        zeroth, first = edge(head), edge(head + 1)
        before_last, last = earlier(tail), earlier(tail + 1)
        a, b, c = channel_taps(tables_ref, modes, j)
        return a * zeroth + b * last + c * before_last, a * first + b * zeroth + c * last

    key0, key1 = firsts(1, 0, 4)
    value0, value1 = firsts(2, 2, 6)
    product0, product1 = key0 * value0, key1 * value1
    for k, array in enumerate((product0, product1)):
        firsts_ref[pl.ds(k * blocks, blocks), :] = array
    own_product0, own_product1 = (firsts_ref[pl.ds(k * blocks + own, 1), :] for k in range(2))
    before = edge_ref[...].astype(jnp.float32)
    before_last, last = before[EDGE - 2 : EDGE - 1], before[EDGE - 1 : EDGE]
    _, b, c = channel_taps(tables_ref, modes, 0)
    own_query0 = local_ref[pl.ds(0, 1), :] + b * last + c * before_last
    own_query1 = local_ref[pl.ds(1, 1), :] + c * last

    state = jnp.zeros((modes, width), jnp.float32)
    for e in range(blocks - 1):
        end = [recv_ref[e, pl.ds(t * modes, modes), :].astype(jnp.float32) for t in range(tiles)]
        added = (
            jnp.concatenate(end, 1)
            + weight0 * product0[e : e + 1]
            + weight1 * product1[e : e + 1]
        )
        state = jnp.where(e < own, state * over_block + added, state)

    state0 = decay * state + own_product0
    state1 = decay * state0 + own_product1
    gated0, gated1 = (
        q * (jnp.sum(coef * h, 0, keepdims=True) + skip * p)
        for q, h, p in (
            (own_query0, state0, own_product0), (own_query1, state1, own_product1)
        )
    )

    start = coef * (state + grow * (own_product0 + grow * own_product1))
    for j in range(CHUNKS):
        for t in range(width // LANES):
            where = pl.ds(t * modes * CHUNKS + j, modes, stride=CHUNKS)
            states_ref[where, :] = start[:, t * LANES : (t + 1) * LANES]
        start = start * over_chunk
    for t in range(width // LANES):
        part = [spread(decay, r, t) for r in range(modes)]
        begin = tuple(
            states_ref[pl.ds((t * modes + r) * CHUNKS, CHUNKS), :] for r in range(modes)
        )

        def step(i, carry, t=t, part=part):
            carry = tuple(d * h for d, h in zip(part, carry))
            where = pl.ds(t * rows + i, CHUNKS, stride=steps)
            conv_ref[where, :] = functools.reduce(jnp.add, carry)
            return carry

        lax.fori_loop(0, steps, step, begin, unroll=4)
    query, base = local_ref[pl.ds(0, rows), :], local_ref[pl.ds(rows, rows), :]
    gated = base + query * whole(conv_ref, rows, width)
    row = lax.broadcasted_iota(jnp.int32, (rows, width), 0)
    gated = jnp.where(row == 0, gated0, jnp.where(row == 1, gated1, gated))
    gated = gated.astype(jnp.bfloat16).astype(jnp.float32)
    root = jnp.sqrt(jnp.sqrt(jnp.abs(gated) * 2.0**32))
    out_ref[...] = jnp.where(gated < 0.0, -root, root)


def shards(features, short_taps, residues, rates, skip, out_weight):
    blocks = lax.axis_size("ctx")
    rows, _, width = features.shape
    modes = rates.shape[0]
    feats = features.transpose(1, 0, 2)
    skip = skip.reshape(1, width)
    f32 = jnp.float32
    tiles = width // LANES
    payload = tiles * (modes + RIM)
    plane = jax.ShapeDtypeStruct((rows, width), f32)
    by_row = pltpu.VMEM((tiles * rows, LANES), f32)
    by_mode = pltpu.VMEM((tiles * modes * CHUNKS, LANES), f32)
    whole_in = pl.BlockSpec(memory_space=pltpu.VMEM)
    sent, edge, tables = pl.pallas_call(
        state_kernel,
        in_specs=[pl.BlockSpec(memory_space=pltpu.HBM)] * 5,
        out_specs=(whole_in,) * 3,
        out_shape=(
            jax.ShapeDtypeStruct((blocks, payload, LANES), jnp.bfloat16),
            jax.ShapeDtypeStruct((EDGE, width), jnp.bfloat16),
            jax.ShapeDtypeStruct(((TABLES + 1) * modes, width), f32),
        ),
        scratch_shapes=[
            pltpu.VMEM(feats.shape, feats.dtype),
            pltpu.VMEM(short_taps.shape, f32),
            pltpu.VMEM(rates.shape, f32),
            pltpu.VMEM(residues.shape, f32),
            pltpu.VMEM(skip.shape, f32),
            by_row,
            by_mode,
            pltpu.SemaphoreType.DMA((5,)),
        ],
        name="block_state",
    )(feats, short_taps, rates, residues, skip)
    received = lax.all_to_all(sent, "ctx", split_axis=0, concat_axis=0, tiled=True)
    before = lax.ppermute(edge, "ctx", [(i, i + 1) for i in range(blocks - 1)])
    local = pl.pallas_call(
        local_kernel,
        in_specs=[whole_in] * 2,
        out_specs=whole_in,
        out_shape=jax.ShapeDtypeStruct((2 * rows + (TABLES + 1) * modes, width), f32),
        scratch_shapes=[by_row, by_mode, by_row],
        compiler_params=pltpu.CompilerParams(vmem_limit_bytes=KERNEL_VMEM),
        name="local_conv",
    )(feats, tables)
    coded = pl.pallas_call(
        carry_kernel,
        in_specs=[whole_in] * 3,
        out_specs=whole_in,
        out_shape=plane,
        scratch_shapes=[
            pltpu.VMEM((tiles * blocks * RIM, LANES), f32),
            pltpu.VMEM((2 * blocks, width), f32),
            by_mode,
            by_row,
        ],
        compiler_params=pltpu.CompilerParams(vmem_limit_bytes=KERNEL_VMEM),
        name="carry_gate",
    )(received, before, local)
    gathered = lax.all_gather(coded.astype(jnp.float16), "tp", axis=1, tiled=True).astype(f32)
    square = gathered * gathered
    gated = (square * (gathered * jnp.abs(gathered))).astype(jnp.bfloat16)
    mixed = jnp.dot(gated, out_weight, preferred_element_type=f32)
    return (mixed * 2.0**-32).astype(jnp.bfloat16)


def solution(mesh):
    in_specs = (
        P("ctx", None, "tp"),
        P(None, None, "tp"),
        P(None, "tp"),
        P(None, "tp"),
        P("tp"),
        P(None, "tp"),
    )
    return jax.shard_map(
        shards, mesh=mesh, in_specs=in_specs, out_specs=P("ctx", "tp"), check_vma=False
    )
```

```python
import functools

import jax
import jax.numpy as jnp
from jax import lax
from jax.experimental import pallas as pl
from jax.experimental.pallas import tpu as pltpu
from jax.sharding import PartitionSpec as P

SHORT = 3
CHUNKS = 8
RIM = 8
EDGE = 16
LANES = 128
TABLES = 7
KERNEL_VMEM = 12 * 2**20
HIGHEST = lax.Precision.HIGHEST


def per_channel(table, width):
    filters = table.shape[1]
    group = width // filters
    row = lax.broadcasted_iota(jnp.int32, (filters, width), 0)
    col = lax.broadcasted_iota(jnp.int32, (filters, width), 1)
    pick = jnp.where(col // group == row, 1.0, 0.0).astype(jnp.float32)
    return lax.dot_general(
        table, pick, (((1,), (0,)), ((), ())), precision=HIGHEST,
        preferred_element_type=jnp.float32,
    )


def short_filter(block, taps, before_last, last):
    row = lax.broadcasted_iota(jnp.int32, block.shape, 0)
    one = jnp.where(row == 0, last, pltpu.roll(block, 1, 0))
    two = jnp.where(row == 0, before_last, jnp.where(row == 1, last, pltpu.roll(block, 2, 0)))
    return taps[0] * block + taps[1] * one + taps[2] * two


def save(ref, array):
    rows, width = array.shape
    for t in range(width // LANES):
        ref[pl.ds(t * rows, rows), :] = array[:, t * LANES : (t + 1) * LANES]


def strided(ref, rows, width, start, count, stride):
    return jnp.concatenate(
        [ref[pl.ds(t * rows + start, count, stride=stride), :] for t in range(width // LANES)], 1
    )


def whole(ref, rows, width):
    return jnp.concatenate([ref[pl.ds(t * rows, rows), :] for t in range(width // LANES)], 1)


def spread(table, r, t):
    return jnp.broadcast_to(table[r : r + 1, t * LANES : (t + 1) * LANES], (CHUNKS, LANES))


def recur(product_ref, base, decay, states, steps, visit=None):
    def step(i, carry):
        now = product_ref[pl.ds(base + i, CHUNKS, stride=steps), :]
        carry = tuple(d * h + now for d, h in zip(decay, carry))
        if visit is not None:
            visit(i, carry)
        return carry

    return lax.fori_loop(0, steps, step, states, unroll=16)


def chunk_ends(product_ref, ends_ref, decay, rows):
    modes, width = decay.shape
    for t in range(width // LANES):
        blank = tuple(jnp.zeros((CHUNKS, LANES), jnp.float32) for _ in range(modes))
        part = [spread(decay, r, t) for r in range(modes)]
        ends = recur(product_ref, t * rows, part, blank, rows // CHUNKS)
        for r, end in enumerate(ends):
            ends_ref[pl.ds((t * modes + r) * CHUNKS, CHUNKS), :] = end


def table(tables_ref, modes, k):
    return tables_ref[pl.ds(k * modes, modes), :]


def single(tables_ref, modes, k):
    return tables_ref[pl.ds(TABLES * modes + k, 1), :]


def channel_taps(tables_ref, modes, j):
    return [single(tables_ref, modes, SHORT * j + shift) for shift in range(SHORT)]


def inner_product(feat_ref, tables_ref, modes):
    rows, width = feat_ref.shape[1:]
    zero = jnp.zeros((1, width), jnp.float32)
    keys, values = (
        short_filter(
            feat_ref[j].astype(jnp.float32), channel_taps(tables_ref, modes, j), zero, zero
        )
        for j in (1, 2)
    )
    row = lax.broadcasted_iota(jnp.int32, (rows, width), 0)
    return jnp.where(row < SHORT - 1, 0.0, keys * values)


def state_kernel(
    feat_hbm, taps_hbm, rates_hbm, residues_hbm, skip_hbm, send_ref, edge_ref, tables_ref,
    feat_ref, taps_ref, rates_ref, residues_ref, skip_ref, product_ref, ends_ref, sems,
):
    copies = [
        pltpu.make_async_copy(source, target, sems.at[k])
        for k, (source, target) in enumerate(
            (
                (rates_hbm, rates_ref), (residues_hbm, residues_ref), (taps_hbm, taps_ref),
                (skip_hbm, skip_ref), (feat_hbm, feat_ref),
            )
        )
    ]
    for copy in copies:
        copy.start()
    rows, width = feat_ref.shape[1:]
    modes = rates_ref.shape[0]
    steps = rows // CHUNKS
    copies[0].wait()
    copies[1].wait()
    rates = rates_ref[...]
    lam = per_channel(rates, width)
    decay = jnp.exp(-lam)
    over_chunk = jnp.exp(-lam * float(steps))
    coef = per_channel(residues_ref[...] * jnp.sqrt(2.0 * rates), width)
    for k, values in enumerate(
        (
            decay,
            jnp.exp(lam),
            jnp.exp(-lam * float(rows - 2)),
            jnp.exp(-lam * float(rows - 1)),
            jnp.exp(-lam * float(rows)),
            over_chunk,
            coef,
        )
    ):
        tables_ref[pl.ds(k * modes, modes), :] = values
    copies[2].wait()
    copies[3].wait()
    taps = [taps_ref[shift, j : j + 1, :] for j in range(3) for shift in range(SHORT)]
    unused = [jnp.zeros((modes - 3 * SHORT - 1, width), jnp.float32)]
    tables_ref[pl.ds(TABLES * modes, modes), :] = jnp.concatenate(
        taps + [skip_ref[...]] + unused, 0
    )
    copies[4].wait()
    save(product_ref, inner_product(feat_ref, tables_ref, modes))
    chunk_ends(product_ref, ends_ref, decay, rows)
    total = jnp.zeros((modes, width), jnp.float32)
    for j in range(CHUNKS):
        end = strided(ends_ref, modes * CHUNKS, width, j, modes, CHUNKS)
        total = total * over_chunk + end
    edges = [
        feat_ref[j, pl.ds(first, EDGE), :].astype(jnp.float32)[at : at + 2]
        for first, at in ((0, 0), (rows - EDGE, EDGE - 2))
        for j in (1, 2)
    ]
    edges = jnp.concatenate(edges, 0)
    block = jnp.concatenate(
        [a[:, t * LANES : (t + 1) * LANES] for a in (total, edges) for t in range(width // LANES)], 0
    )
    block = block.astype(jnp.bfloat16)
    edge_ref[...] = feat_ref[0, pl.ds(rows - EDGE, EDGE), :]
    for e in range(send_ref.shape[0]):
        send_ref[e] = block


def local_kernel(feat_ref, tables_ref, local_ref, product_ref, states_ref, conv_ref):
    rows, width = feat_ref.shape[1:]
    modes = tables_ref.shape[0] // (TABLES + 1)
    steps = rows // CHUNKS
    decay, over_chunk, coef = (table(tables_ref, modes, k) for k in (0, 5, 6))
    zero = jnp.zeros((1, width), jnp.float32)
    query = short_filter(
        feat_ref[0].astype(jnp.float32), channel_taps(tables_ref, modes, 0), zero, zero
    )
    product = inner_product(feat_ref, tables_ref, modes)
    save(product_ref, product)
    chunk_ends(product_ref, states_ref, decay, rows)
    state = jnp.zeros((modes, width), jnp.float32)
    for j in range(CHUNKS):
        end = strided(states_ref, modes * CHUNKS, width, j, modes, CHUNKS)
        for t in range(width // LANES):
            where = pl.ds(t * modes * CHUNKS + j, modes, stride=CHUNKS)
            states_ref[where, :] = state[:, t * LANES : (t + 1) * LANES]
        state = state * over_chunk + end
    for t in range(width // LANES):
        part = [spread(decay, r, t) for r in range(modes)]
        scale = [spread(coef, r, t) for r in range(modes)]
        begin = tuple(
            states_ref[pl.ds((t * modes + r) * CHUNKS, CHUNKS), :] for r in range(modes)
        )

        def visit(i, carry, t=t, scale=scale):
            total = functools.reduce(jnp.add, [s * h for s, h in zip(scale, carry)])
            conv_ref[pl.ds(t * rows + i, CHUNKS, stride=steps), :] = total

        recur(product_ref, t * rows, part, begin, steps, visit)
    skip = single(tables_ref, modes, 3 * SHORT)
    local_ref[pl.ds(2 * rows, (TABLES + 1) * modes), :] = tables_ref[...]
    local_ref[pl.ds(0, rows), :] = query
    local_ref[pl.ds(rows, rows), :] = query * (whole(conv_ref, rows, width) + skip * product)


def carry_kernel(
    recv_ref, edge_ref, local_ref, out_ref,
    rims_ref, firsts_ref, states_ref, conv_ref,
):
    blocks = recv_ref.shape[0]
    rows, width = out_ref.shape
    tiles = width // LANES
    modes = recv_ref.shape[1] // tiles - RIM
    steps = rows // CHUNKS
    own = lax.axis_index("ctx")
    tables_ref = local_ref.at[pl.ds(2 * rows, (TABLES + 1) * modes)]
    decay, grow, weight1, weight0, over_block, over_chunk, coef = (
        table(tables_ref, modes, k) for k in range(TABLES)
    )
    skip = single(tables_ref, modes, 3 * SHORT)

    for e in range(blocks):
        edges = recv_ref[e, pl.ds(tiles * modes, tiles * RIM), :].astype(jnp.float32)
        rims_ref[pl.ds(e * tiles * RIM, tiles * RIM), :] = edges

    def edge(k):
        return strided(rims_ref, RIM, width, k, blocks, tiles * RIM)

    block_row = lax.broadcasted_iota(jnp.int32, (blocks, width), 0)

    def earlier(k):
        return jnp.where(block_row == 0, 0.0, pltpu.roll(edge(k), 1, 0))

    def firsts(j, head, tail):
        zeroth, first = edge(head), edge(head + 1)
        before_last, last = earlier(tail), earlier(tail + 1)
        a, b, c = channel_taps(tables_ref, modes, j)
        return a * zeroth + b * last + c * before_last, a * first + b * zeroth + c * last

    key0, key1 = firsts(1, 0, 4)
    value0, value1 = firsts(2, 2, 6)
    product0, product1 = key0 * value0, key1 * value1
    for k, array in enumerate((product0, product1)):
        firsts_ref[pl.ds(k * blocks, blocks), :] = array
    own_product0, own_product1 = (firsts_ref[pl.ds(k * blocks + own, 1), :] for k in range(2))
    before = edge_ref[...].astype(jnp.float32)
    before_last, last = before[EDGE - 2 : EDGE - 1], before[EDGE - 1 : EDGE]
    _, b, c = channel_taps(tables_ref, modes, 0)
    own_query0 = local_ref[pl.ds(0, 1), :] + b * last + c * before_last
    own_query1 = local_ref[pl.ds(1, 1), :] + c * last

    state = jnp.zeros((modes, width), jnp.float32)
    for e in range(blocks - 1):
        end = [recv_ref[e, pl.ds(t * modes, modes), :].astype(jnp.float32) for t in range(tiles)]
        added = (
            jnp.concatenate(end, 1)
            + weight0 * product0[e : e + 1]
            + weight1 * product1[e : e + 1]
        )
        state = jnp.where(e < own, state * over_block + added, state)

    state0 = decay * state + own_product0
    state1 = decay * state0 + own_product1
    gated0, gated1 = (
        q * (jnp.sum(coef * h, 0, keepdims=True) + skip * p)
        for q, h, p in (
            (own_query0, state0, own_product0), (own_query1, state1, own_product1)
        )
    )

    start = coef * (state + grow * (own_product0 + grow * own_product1))
    for j in range(CHUNKS):
        for t in range(width // LANES):
            where = pl.ds(t * modes * CHUNKS + j, modes, stride=CHUNKS)
            states_ref[where, :] = start[:, t * LANES : (t + 1) * LANES]
        start = start * over_chunk
    for t in range(width // LANES):
        part = [spread(decay, r, t) for r in range(modes)]
        begin = tuple(
            states_ref[pl.ds((t * modes + r) * CHUNKS, CHUNKS), :] for r in range(modes)
        )

        def step(i, carry, t=t, part=part):
            carry = tuple(d * h for d, h in zip(part, carry))
            where = pl.ds(t * rows + i, CHUNKS, stride=steps)
            conv_ref[where, :] = functools.reduce(jnp.add, carry)
            return carry

        lax.fori_loop(0, steps, step, begin, unroll=4)
    query, base = local_ref[pl.ds(0, rows), :], local_ref[pl.ds(rows, rows), :]
    gated = base + query * whole(conv_ref, rows, width)
    row = lax.broadcasted_iota(jnp.int32, (rows, width), 0)
    gated = jnp.where(row == 0, gated0, jnp.where(row == 1, gated1, gated))
    gated = gated.astype(jnp.bfloat16).astype(jnp.float32)
    root = jnp.sqrt(jnp.sqrt(jnp.abs(gated) * 2.0**32))
    out_ref[...] = jnp.where(gated < 0.0, -root, root)


def shards(features, short_taps, residues, rates, skip, out_weight):
    blocks = lax.axis_size("ctx")
    rows, _, width = features.shape
    modes = rates.shape[0]
    feats = features.transpose(1, 0, 2)
    skip = skip.reshape(1, width)
    f32 = jnp.float32
    tiles = width // LANES
    payload = tiles * (modes + RIM)
    plane = jax.ShapeDtypeStruct((rows, width), f32)
    by_row = pltpu.VMEM((tiles * rows, LANES), f32)
    by_mode = pltpu.VMEM((tiles * modes * CHUNKS, LANES), f32)
    whole_in = pl.BlockSpec(memory_space=pltpu.VMEM)
    sent, edge, tables = pl.pallas_call(
        state_kernel,
        in_specs=[pl.BlockSpec(memory_space=pltpu.HBM)] * 5,
        out_specs=(whole_in,) * 3,
        out_shape=(
            jax.ShapeDtypeStruct((blocks, payload, LANES), jnp.bfloat16),
            jax.ShapeDtypeStruct((EDGE, width), jnp.bfloat16),
            pltpu.VMEM(((TABLES + 1) * modes, width), f32),
        ),
        scratch_shapes=[
            pltpu.VMEM(feats.shape, feats.dtype),
            pltpu.VMEM(short_taps.shape, f32),
            pltpu.VMEM(rates.shape, f32),
            pltpu.VMEM(residues.shape, f32),
            pltpu.VMEM(skip.shape, f32),
            by_row,
            by_mode,
            pltpu.SemaphoreType.DMA((5,)),
        ],
        name="block_state",
    )(feats, short_taps, rates, residues, skip)
    received = lax.all_to_all(sent, "ctx", split_axis=0, concat_axis=0, tiled=True)
    before = lax.ppermute(edge, "ctx", [(i, i + 1) for i in range(blocks - 1)])
    local = pl.pallas_call(
        local_kernel,
        in_specs=[whole_in] * 2,
        out_specs=whole_in,
        out_shape=jax.ShapeDtypeStruct((2 * rows + (TABLES + 1) * modes, width), f32),
        scratch_shapes=[by_row, by_mode, by_row],
        compiler_params=pltpu.CompilerParams(vmem_limit_bytes=KERNEL_VMEM),
        name="local_conv",
    )(feats, tables)
    coded = pl.pallas_call(
        carry_kernel,
        in_specs=[whole_in] * 3,
        out_specs=whole_in,
        out_shape=plane,
        scratch_shapes=[
            pltpu.VMEM((tiles * blocks * RIM, LANES), f32),
            pltpu.VMEM((2 * blocks, width), f32),
            by_mode,
            by_row,
        ],
        compiler_params=pltpu.CompilerParams(vmem_limit_bytes=KERNEL_VMEM),
        name="carry_gate",
    )(received, before, local)
    gathered = lax.all_gather(coded.astype(jnp.float16), "tp", axis=1, tiled=True).astype(f32)
    square = gathered * gathered
    gated = (square * (gathered * jnp.abs(gathered))).astype(jnp.bfloat16)
    mixed = jnp.dot(gated, out_weight, preferred_element_type=f32)
    return (mixed * 2.0**-32).astype(jnp.bfloat16)


def solution(mesh):
    in_specs = (
        P("ctx", None, "tp"),
        P(None, None, "tp"),
        P(None, "tp"),
        P(None, "tp"),
        P("tp"),
        P(None, "tp"),
    )
    return jax.shard_map(
        shards, mesh=mesh, in_specs=in_specs, out_specs=P("ctx", "tp"), check_vma=False
    )
```

```python
import functools

import jax
import jax.numpy as jnp
from jax import lax
from jax.experimental import pallas as pl
from jax.experimental.pallas import tpu as pltpu
from jax.sharding import PartitionSpec as P

SHORT = 3
CHUNKS = 8
RIM = 8
EDGE = 16
LANES = 128
TABLES = 7
KERNEL_VMEM = 12 * 2**20
HIGHEST = lax.Precision.HIGHEST


def per_channel(table, width):
    filters = table.shape[1]
    group = width // filters
    row = lax.broadcasted_iota(jnp.int32, (filters, width), 0)
    col = lax.broadcasted_iota(jnp.int32, (filters, width), 1)
    pick = jnp.where(col // group == row, 1.0, 0.0).astype(jnp.float32)
    return lax.dot_general(
        table, pick, (((1,), (0,)), ((), ())), precision=HIGHEST,
        preferred_element_type=jnp.float32,
    )


def short_filter(block, taps, before_last, last):
    row = lax.broadcasted_iota(jnp.int32, block.shape, 0)
    one = jnp.where(row == 0, last, pltpu.roll(block, 1, 0))
    two = jnp.where(row == 0, before_last, jnp.where(row == 1, last, pltpu.roll(block, 2, 0)))
    return taps[0] * block + taps[1] * one + taps[2] * two


def save(ref, array):
    rows, width = array.shape
    for t in range(width // LANES):
        ref[pl.ds(t * rows, rows), :] = array[:, t * LANES : (t + 1) * LANES]


def strided(ref, rows, width, start, count, stride):
    return jnp.concatenate(
        [ref[pl.ds(t * rows + start, count, stride=stride), :] for t in range(width // LANES)], 1
    )


def whole(ref, rows, width):
    return jnp.concatenate([ref[pl.ds(t * rows, rows), :] for t in range(width // LANES)], 1)


def spread(table, r, t):
    return jnp.broadcast_to(table[r : r + 1, t * LANES : (t + 1) * LANES], (CHUNKS, LANES))


def recur(product_ref, base, decay, states, steps, visit=None):
    def step(i, carry):
        now = product_ref[pl.ds(base + i, CHUNKS, stride=steps), :]
        carry = tuple(d * h + now for d, h in zip(decay, carry))
        if visit is not None:
            visit(i, carry)
        return carry

    return lax.fori_loop(0, steps, step, states, unroll=16)


def chunk_ends(product_ref, ends_ref, decay, rows):
    modes, width = decay.shape
    for t in range(width // LANES):
        blank = tuple(jnp.zeros((CHUNKS, LANES), jnp.float32) for _ in range(modes))
        part = [spread(decay, r, t) for r in range(modes)]
        ends = recur(product_ref, t * rows, part, blank, rows // CHUNKS)
        for r, end in enumerate(ends):
            ends_ref[pl.ds((t * modes + r) * CHUNKS, CHUNKS), :] = end


def table(tables_ref, modes, k):
    return tables_ref[pl.ds(k * modes, modes), :]


def single(tables_ref, modes, k):
    return tables_ref[pl.ds(TABLES * modes + k, 1), :]


def channel_taps(tables_ref, modes, j):
    return [single(tables_ref, modes, SHORT * j + shift) for shift in range(SHORT)]


def inner_product(feat_ref, tables_ref, modes):
    rows, width = feat_ref.shape[1:]
    zero = jnp.zeros((1, width), jnp.float32)
    keys, values = (
        short_filter(
            feat_ref[j].astype(jnp.float32), channel_taps(tables_ref, modes, j), zero, zero
        )
        for j in (1, 2)
    )
    row = lax.broadcasted_iota(jnp.int32, (rows, width), 0)
    return jnp.where(row < SHORT - 1, 0.0, keys * values)


def split(array):
    head = array.astype(jnp.bfloat16)
    return head, (array - head.astype(jnp.float32)).astype(jnp.bfloat16)


def weigh(left, right):
    return jnp.dot(left, right, preferred_element_type=jnp.float32)


def state_kernel(
    feat_hbm, taps_hbm, rates_hbm, residues_hbm, skip_hbm, send_ref, edge_ref, tables_ref,
    feat_ref, taps_ref, rates_ref, residues_ref, skip_ref, sems,
):
    copies = [
        pltpu.make_async_copy(source, target, sems.at[k])
        for k, (source, target) in enumerate(
            (
                (rates_hbm, rates_ref), (residues_hbm, residues_ref), (taps_hbm, taps_ref),
                (skip_hbm, skip_ref), (feat_hbm, feat_ref),
            )
        )
    ]
    for copy in copies:
        copy.start()
    rows, width = feat_ref.shape[1:]
    modes = rates_ref.shape[0]
    steps = rows // CHUNKS
    copies[0].wait()
    copies[1].wait()
    rates = rates_ref[...]
    lam = per_channel(rates, width)
    decay = jnp.exp(-lam)
    over_chunk = jnp.exp(-lam * float(steps))
    coef = per_channel(residues_ref[...] * jnp.sqrt(2.0 * rates), width)
    for k, values in enumerate(
        (
            decay,
            jnp.exp(lam),
            jnp.exp(-lam * float(rows - 2)),
            jnp.exp(-lam * float(rows - 1)),
            jnp.exp(-lam * float(rows)),
            over_chunk,
            coef,
        )
    ):
        tables_ref[pl.ds(k * modes, modes), :] = values
    filters = rates.shape[1]
    column = jnp.concatenate([rates[:, f : f + 1] for f in range(filters)], 0)
    age = rows - 1 - lax.broadcasted_iota(jnp.int32, (filters * modes, rows), 1)
    weights, weights_rest = split(jnp.exp(-column * age.astype(jnp.float32)))
    copies[2].wait()
    copies[3].wait()
    taps = [taps_ref[shift, j : j + 1, :] for j in range(3) for shift in range(SHORT)]
    unused = [jnp.zeros((modes - 3 * SHORT - 1, width), jnp.float32)]
    tables_ref[pl.ds(TABLES * modes, modes), :] = jnp.concatenate(
        taps + [skip_ref[...]] + unused, 0
    )
    copies[4].wait()
    product, product_rest = split(inner_product(feat_ref, tables_ref, modes))
    every = weigh(weights, product) + (weigh(weights, product_rest) + weigh(weights_rest, product))
    owner = lax.broadcasted_iota(jnp.int32, (modes, width), 1) // (width // filters)
    total = jnp.zeros((modes, width), jnp.float32)
    for f in range(filters):
        total = jnp.where(owner == f, every[f * modes : (f + 1) * modes], total)
    edges = [
        feat_ref[j, pl.ds(first, EDGE), :].astype(jnp.float32)[at : at + 2]
        for first, at in ((0, 0), (rows - EDGE, EDGE - 2))
        for j in (1, 2)
    ]
    edges = jnp.concatenate(edges, 0)
    block = jnp.concatenate(
        [a[:, t * LANES : (t + 1) * LANES] for a in (total, edges) for t in range(width // LANES)], 0
    )
    block = block.astype(jnp.bfloat16)
    edge_ref[...] = feat_ref[0, pl.ds(rows - EDGE, EDGE), :]
    for e in range(send_ref.shape[0]):
        send_ref[e] = block


def local_kernel(feat_ref, tables_ref, local_ref, product_ref, states_ref, conv_ref):
    rows, width = feat_ref.shape[1:]
    modes = tables_ref.shape[0] // (TABLES + 1)
    steps = rows // CHUNKS
    decay, over_chunk, coef = (table(tables_ref, modes, k) for k in (0, 5, 6))
    zero = jnp.zeros((1, width), jnp.float32)
    query = short_filter(
        feat_ref[0].astype(jnp.float32), channel_taps(tables_ref, modes, 0), zero, zero
    )
    product = inner_product(feat_ref, tables_ref, modes)
    save(product_ref, product)
    chunk_ends(product_ref, states_ref, decay, rows)
    state = jnp.zeros((modes, width), jnp.float32)
    for j in range(CHUNKS):
        end = strided(states_ref, modes * CHUNKS, width, j, modes, CHUNKS)
        for t in range(width // LANES):
            where = pl.ds(t * modes * CHUNKS + j, modes, stride=CHUNKS)
            states_ref[where, :] = state[:, t * LANES : (t + 1) * LANES]
        state = state * over_chunk + end
    for t in range(width // LANES):
        part = [spread(decay, r, t) for r in range(modes)]
        scale = [spread(coef, r, t) for r in range(modes)]
        begin = tuple(
            states_ref[pl.ds((t * modes + r) * CHUNKS, CHUNKS), :] for r in range(modes)
        )

        def visit(i, carry, t=t, scale=scale):
            total = functools.reduce(jnp.add, [s * h for s, h in zip(scale, carry)])
            conv_ref[pl.ds(t * rows + i, CHUNKS, stride=steps), :] = total

        recur(product_ref, t * rows, part, begin, steps, visit)
    skip = single(tables_ref, modes, 3 * SHORT)
    local_ref[pl.ds(2 * rows, (TABLES + 1) * modes), :] = tables_ref[...]
    local_ref[pl.ds(0, rows), :] = query
    local_ref[pl.ds(rows, rows), :] = query * (whole(conv_ref, rows, width) + skip * product)


def carry_kernel(
    recv_ref, edge_ref, local_ref, out_ref,
    rims_ref, firsts_ref, states_ref, conv_ref,
):
    blocks = recv_ref.shape[0]
    rows, width = out_ref.shape
    tiles = width // LANES
    modes = recv_ref.shape[1] // tiles - RIM
    steps = rows // CHUNKS
    own = lax.axis_index("ctx")
    tables_ref = local_ref.at[pl.ds(2 * rows, (TABLES + 1) * modes)]
    decay, grow, weight1, weight0, over_block, over_chunk, coef = (
        table(tables_ref, modes, k) for k in range(TABLES)
    )
    skip = single(tables_ref, modes, 3 * SHORT)

    for e in range(blocks):
        edges = recv_ref[e, pl.ds(tiles * modes, tiles * RIM), :].astype(jnp.float32)
        rims_ref[pl.ds(e * tiles * RIM, tiles * RIM), :] = edges

    def edge(k):
        return strided(rims_ref, RIM, width, k, blocks, tiles * RIM)

    block_row = lax.broadcasted_iota(jnp.int32, (blocks, width), 0)

    def earlier(k):
        return jnp.where(block_row == 0, 0.0, pltpu.roll(edge(k), 1, 0))

    def firsts(j, head, tail):
        zeroth, first = edge(head), edge(head + 1)
        before_last, last = earlier(tail), earlier(tail + 1)
        a, b, c = channel_taps(tables_ref, modes, j)
        return a * zeroth + b * last + c * before_last, a * first + b * zeroth + c * last

    key0, key1 = firsts(1, 0, 4)
    value0, value1 = firsts(2, 2, 6)
    product0, product1 = key0 * value0, key1 * value1
    for k, array in enumerate((product0, product1)):
        firsts_ref[pl.ds(k * blocks, blocks), :] = array
    own_product0, own_product1 = (firsts_ref[pl.ds(k * blocks + own, 1), :] for k in range(2))
    before = edge_ref[...].astype(jnp.float32)
    before_last, last = before[EDGE - 2 : EDGE - 1], before[EDGE - 1 : EDGE]
    _, b, c = channel_taps(tables_ref, modes, 0)
    own_query0 = local_ref[pl.ds(0, 1), :] + b * last + c * before_last
    own_query1 = local_ref[pl.ds(1, 1), :] + c * last

    state = jnp.zeros((modes, width), jnp.float32)
    for e in range(blocks - 1):
        end = [recv_ref[e, pl.ds(t * modes, modes), :].astype(jnp.float32) for t in range(tiles)]
        added = (
            jnp.concatenate(end, 1)
            + weight0 * product0[e : e + 1]
            + weight1 * product1[e : e + 1]
        )
        state = jnp.where(e < own, state * over_block + added, state)

    state0 = decay * state + own_product0
    state1 = decay * state0 + own_product1
    gated0, gated1 = (
        q * (jnp.sum(coef * h, 0, keepdims=True) + skip * p)
        for q, h, p in (
            (own_query0, state0, own_product0), (own_query1, state1, own_product1)
        )
    )

    start = coef * (state + grow * (own_product0 + grow * own_product1))
    for j in range(CHUNKS):
        for t in range(width // LANES):
            where = pl.ds(t * modes * CHUNKS + j, modes, stride=CHUNKS)
            states_ref[where, :] = start[:, t * LANES : (t + 1) * LANES]
        start = start * over_chunk
    for t in range(width // LANES):
        part = [spread(decay, r, t) for r in range(modes)]
        begin = tuple(
            states_ref[pl.ds((t * modes + r) * CHUNKS, CHUNKS), :] for r in range(modes)
        )

        def step(i, carry, t=t, part=part):
            carry = tuple(d * h for d, h in zip(part, carry))
            where = pl.ds(t * rows + i, CHUNKS, stride=steps)
            conv_ref[where, :] = functools.reduce(jnp.add, carry)
            return carry

        lax.fori_loop(0, steps, step, begin, unroll=4)
    query, base = local_ref[pl.ds(0, rows), :], local_ref[pl.ds(rows, rows), :]
    gated = base + query * whole(conv_ref, rows, width)
    row = lax.broadcasted_iota(jnp.int32, (rows, width), 0)
    gated = jnp.where(row == 0, gated0, jnp.where(row == 1, gated1, gated))
    gated = gated.astype(jnp.bfloat16).astype(jnp.float32)
    root = jnp.sqrt(jnp.sqrt(jnp.abs(gated) * 2.0**32))
    out_ref[...] = jnp.where(gated < 0.0, -root, root)


def shards(features, short_taps, residues, rates, skip, out_weight):
    blocks = lax.axis_size("ctx")
    rows, _, width = features.shape
    modes = rates.shape[0]
    feats = features.transpose(1, 0, 2)
    skip = skip.reshape(1, width)
    f32 = jnp.float32
    tiles = width // LANES
    payload = tiles * (modes + RIM)
    plane = jax.ShapeDtypeStruct((rows, width), f32)
    by_row = pltpu.VMEM((tiles * rows, LANES), f32)
    by_mode = pltpu.VMEM((tiles * modes * CHUNKS, LANES), f32)
    whole_in = pl.BlockSpec(memory_space=pltpu.VMEM)
    sent, edge, tables = pl.pallas_call(
        state_kernel,
        in_specs=[pl.BlockSpec(memory_space=pltpu.HBM)] * 5,
        out_specs=(whole_in,) * 3,
        out_shape=(
            jax.ShapeDtypeStruct((blocks, payload, LANES), jnp.bfloat16),
            jax.ShapeDtypeStruct((EDGE, width), jnp.bfloat16),
            pltpu.VMEM(((TABLES + 1) * modes, width), f32),
        ),
        scratch_shapes=[
            pltpu.VMEM(feats.shape, feats.dtype),
            pltpu.VMEM(short_taps.shape, f32),
            pltpu.VMEM(rates.shape, f32),
            pltpu.VMEM(residues.shape, f32),
            pltpu.VMEM(skip.shape, f32),
            pltpu.SemaphoreType.DMA((5,)),
        ],
        name="block_state",
    )(feats, short_taps, rates, residues, skip)
    received = lax.all_to_all(sent, "ctx", split_axis=0, concat_axis=0, tiled=True)
    before = lax.ppermute(edge, "ctx", [(i, i + 1) for i in range(blocks - 1)])
    local = pl.pallas_call(
        local_kernel,
        in_specs=[whole_in] * 2,
        out_specs=whole_in,
        out_shape=jax.ShapeDtypeStruct((2 * rows + (TABLES + 1) * modes, width), f32),
        scratch_shapes=[by_row, by_mode, by_row],
        compiler_params=pltpu.CompilerParams(vmem_limit_bytes=KERNEL_VMEM),
        name="local_conv",
    )(feats, tables)
    coded = pl.pallas_call(
        carry_kernel,
        in_specs=[whole_in] * 3,
        out_specs=whole_in,
        out_shape=plane,
        scratch_shapes=[
            pltpu.VMEM((tiles * blocks * RIM, LANES), f32),
            pltpu.VMEM((2 * blocks, width), f32),
            by_mode,
            by_row,
        ],
        compiler_params=pltpu.CompilerParams(vmem_limit_bytes=KERNEL_VMEM),
        name="carry_gate",
    )(received, before, local)
    gathered = lax.all_gather(coded.astype(jnp.float16), "tp", axis=1, tiled=True).astype(f32)
    square = gathered * gathered
    gated = (square * (gathered * jnp.abs(gathered))).astype(jnp.bfloat16)
    mixed = jnp.dot(gated, out_weight, preferred_element_type=f32)
    return (mixed * 2.0**-32).astype(jnp.bfloat16)


def solution(mesh):
    in_specs = (
        P("ctx", None, "tp"),
        P(None, None, "tp"),
        P(None, "tp"),
        P(None, "tp"),
        P("tp"),
        P(None, "tp"),
    )
    return jax.shard_map(
        shards, mesh=mesh, in_specs=in_specs, out_specs=P("ctx", "tp"), check_vma=False
    )
```

```python
import functools

import jax
import jax.numpy as jnp
from jax import lax
from jax.experimental import pallas as pl
from jax.experimental.pallas import tpu as pltpu
from jax.sharding import PartitionSpec as P

SHORT = 3
CHUNKS = 8
RIM = 8
EDGE = 16
LANES = 128
TABLES = 7
KERNEL_VMEM = 12 * 2**20
HIGHEST = lax.Precision.HIGHEST


def per_channel(table, width):
    filters = table.shape[1]
    group = width // filters
    row = lax.broadcasted_iota(jnp.int32, (filters, width), 0)
    col = lax.broadcasted_iota(jnp.int32, (filters, width), 1)
    pick = jnp.where(col // group == row, 1.0, 0.0).astype(jnp.float32)
    return lax.dot_general(
        table, pick, (((1,), (0,)), ((), ())), precision=HIGHEST,
        preferred_element_type=jnp.float32,
    )


def short_filter(block, taps, before_last, last):
    row = lax.broadcasted_iota(jnp.int32, block.shape, 0)
    one = jnp.where(row == 0, last, pltpu.roll(block, 1, 0))
    two = jnp.where(row == 0, before_last, jnp.where(row == 1, last, pltpu.roll(block, 2, 0)))
    return taps[0] * block + taps[1] * one + taps[2] * two


def save(ref, array):
    rows, width = array.shape
    for t in range(width // LANES):
        ref[pl.ds(t * rows, rows), :] = array[:, t * LANES : (t + 1) * LANES]


def strided(ref, rows, width, start, count, stride):
    return jnp.concatenate(
        [ref[pl.ds(t * rows + start, count, stride=stride), :] for t in range(width // LANES)], 1
    )


def whole(ref, rows, width):
    return jnp.concatenate([ref[pl.ds(t * rows, rows), :] for t in range(width // LANES)], 1)


def spread(table, r, t):
    return jnp.broadcast_to(table[r : r + 1, t * LANES : (t + 1) * LANES], (CHUNKS, LANES))


def recur(product_ref, base, decay, states, steps, visit=None):
    def step(i, carry):
        now = product_ref[pl.ds(base + i, CHUNKS, stride=steps), :]
        carry = tuple(d * h + now for d, h in zip(decay, carry))
        if visit is not None:
            visit(i, carry)
        return carry

    return lax.fori_loop(0, steps, step, states, unroll=16)


def chunk_ends(product_ref, ends_ref, decay, rows):
    modes, width = decay.shape
    for t in range(width // LANES):
        blank = tuple(jnp.zeros((CHUNKS, LANES), jnp.float32) for _ in range(modes))
        part = [spread(decay, r, t) for r in range(modes)]
        ends = recur(product_ref, t * rows, part, blank, rows // CHUNKS)
        for r, end in enumerate(ends):
            ends_ref[pl.ds((t * modes + r) * CHUNKS, CHUNKS), :] = end


def table(tables_ref, modes, k):
    return tables_ref[pl.ds(k * modes, modes), :]


def single(tables_ref, modes, k):
    return tables_ref[pl.ds(TABLES * modes + k, 1), :]


def channel_taps(tables_ref, modes, j):
    return [single(tables_ref, modes, SHORT * j + shift) for shift in range(SHORT)]


def inner_product(feat_ref, tables_ref, modes):
    rows, width = feat_ref.shape[1:]
    zero = jnp.zeros((1, width), jnp.float32)
    keys, values = (
        short_filter(
            feat_ref[j].astype(jnp.float32), channel_taps(tables_ref, modes, j), zero, zero
        )
        for j in (1, 2)
    )
    row = lax.broadcasted_iota(jnp.int32, (rows, width), 0)
    return jnp.where(row < SHORT - 1, 0.0, keys * values)


def split(array):
    head = array.astype(jnp.bfloat16)
    return head, (array - head.astype(jnp.float32)).astype(jnp.bfloat16)


def weigh(left, right):
    return jnp.dot(left, right, preferred_element_type=jnp.float32)


def state_kernel(
    feat_hbm, taps_hbm, rates_hbm, residues_hbm, skip_hbm, send_ref, tables_ref,
    feat_ref, taps_ref, rates_ref, residues_ref, skip_ref, sems,
):
    copies = [
        pltpu.make_async_copy(source, target, sems.at[k])
        for k, (source, target) in enumerate(
            (
                (rates_hbm, rates_ref), (residues_hbm, residues_ref), (taps_hbm, taps_ref),
                (skip_hbm, skip_ref), (feat_hbm, feat_ref),
            )
        )
    ]
    for copy in copies:
        copy.start()
    rows, width = feat_ref.shape[1:]
    modes = rates_ref.shape[0]
    steps = rows // CHUNKS
    copies[0].wait()
    copies[1].wait()
    rates = rates_ref[...]
    lam = per_channel(rates, width)
    decay = jnp.exp(-lam)
    over_chunk = jnp.exp(-lam * float(steps))
    coef = per_channel(residues_ref[...] * jnp.sqrt(2.0 * rates), width)
    for k, values in enumerate(
        (
            decay,
            jnp.exp(lam),
            jnp.exp(-lam * float(rows - 2)),
            jnp.exp(-lam * float(rows - 1)),
            jnp.exp(-lam * float(rows)),
            over_chunk,
            coef,
        )
    ):
        tables_ref[pl.ds(k * modes, modes), :] = values
    filters = rates.shape[1]
    column = jnp.concatenate([rates[:, f : f + 1] for f in range(filters)], 0)
    age = rows - 1 - lax.broadcasted_iota(jnp.int32, (filters * modes, rows), 1)
    weights, weights_rest = split(jnp.exp(-column * age.astype(jnp.float32)))
    copies[2].wait()
    copies[3].wait()
    taps = [taps_ref[shift, j : j + 1, :] for j in range(3) for shift in range(SHORT)]
    unused = [jnp.zeros((modes - 3 * SHORT - 1, width), jnp.float32)]
    tables_ref[pl.ds(TABLES * modes, modes), :] = jnp.concatenate(
        taps + [skip_ref[...]] + unused, 0
    )
    copies[4].wait()
    product, product_rest = split(inner_product(feat_ref, tables_ref, modes))
    every = weigh(weights, product) + (weigh(weights, product_rest) + weigh(weights_rest, product))
    owner = lax.broadcasted_iota(jnp.int32, (modes, width), 1) // (width // filters)
    total = jnp.zeros((modes, width), jnp.float32)
    for f in range(filters):
        total = jnp.where(owner == f, every[f * modes : (f + 1) * modes], total)
    edges = [
        feat_ref[j, pl.ds(first, EDGE), :].astype(jnp.float32)[at : at + 2]
        for first, at in ((0, 0), (rows - EDGE, EDGE - 2))
        for j in (1, 2)
    ]
    edges = jnp.concatenate(edges, 0)
    block = jnp.concatenate(
        [a[:, t * LANES : (t + 1) * LANES] for a in (total, edges) for t in range(width // LANES)], 0
    )
    block = block.astype(jnp.bfloat16)
    for e in range(send_ref.shape[0]):
        send_ref[e] = block


def local_kernel(
    feat_ref, tables_ref, local_ref, edge_ref, product_ref, states_ref, conv_ref
):
    rows, width = feat_ref.shape[1:]
    modes = tables_ref.shape[0] // (TABLES + 1)
    steps = rows // CHUNKS
    decay, over_chunk, coef = (table(tables_ref, modes, k) for k in (0, 5, 6))
    zero = jnp.zeros((1, width), jnp.float32)
    query = short_filter(
        feat_ref[0].astype(jnp.float32), channel_taps(tables_ref, modes, 0), zero, zero
    )
    product = inner_product(feat_ref, tables_ref, modes)
    save(product_ref, product)
    chunk_ends(product_ref, states_ref, decay, rows)
    state = jnp.zeros((modes, width), jnp.float32)
    for j in range(CHUNKS):
        end = strided(states_ref, modes * CHUNKS, width, j, modes, CHUNKS)
        for t in range(width // LANES):
            where = pl.ds(t * modes * CHUNKS + j, modes, stride=CHUNKS)
            states_ref[where, :] = state[:, t * LANES : (t + 1) * LANES]
        state = state * over_chunk + end
    for t in range(width // LANES):
        part = [spread(decay, r, t) for r in range(modes)]
        scale = [spread(coef, r, t) for r in range(modes)]
        begin = tuple(
            states_ref[pl.ds((t * modes + r) * CHUNKS, CHUNKS), :] for r in range(modes)
        )

        def visit(i, carry, t=t, scale=scale):
            total = functools.reduce(jnp.add, [s * h for s, h in zip(scale, carry)])
            conv_ref[pl.ds(t * rows + i, CHUNKS, stride=steps), :] = total

        recur(product_ref, t * rows, part, begin, steps, visit)
    skip = single(tables_ref, modes, 3 * SHORT)
    local_ref[pl.ds(2 * rows, (TABLES + 1) * modes), :] = tables_ref[...]
    edge_ref[...] = feat_ref[0, pl.ds(rows - EDGE, EDGE), :]
    local_ref[pl.ds(0, rows), :] = query
    local_ref[pl.ds(rows, rows), :] = query * (whole(conv_ref, rows, width) + skip * product)


def carry_kernel(
    recv_ref, edge_ref, local_ref, out_ref,
    rims_ref, firsts_ref, states_ref, conv_ref,
):
    blocks = recv_ref.shape[0]
    rows, width = out_ref.shape
    tiles = width // LANES
    modes = recv_ref.shape[1] // tiles - RIM
    steps = rows // CHUNKS
    own = lax.axis_index("ctx")
    tables_ref = local_ref.at[pl.ds(2 * rows, (TABLES + 1) * modes)]
    decay, grow, weight1, weight0, over_block, over_chunk, coef = (
        table(tables_ref, modes, k) for k in range(TABLES)
    )
    skip = single(tables_ref, modes, 3 * SHORT)

    for e in range(blocks):
        edges = recv_ref[e, pl.ds(tiles * modes, tiles * RIM), :].astype(jnp.float32)
        rims_ref[pl.ds(e * tiles * RIM, tiles * RIM), :] = edges

    def edge(k):
        return strided(rims_ref, RIM, width, k, blocks, tiles * RIM)

    block_row = lax.broadcasted_iota(jnp.int32, (blocks, width), 0)

    def earlier(k):
        return jnp.where(block_row == 0, 0.0, pltpu.roll(edge(k), 1, 0))

    def firsts(j, head, tail):
        zeroth, first = edge(head), edge(head + 1)
        before_last, last = earlier(tail), earlier(tail + 1)
        a, b, c = channel_taps(tables_ref, modes, j)
        return a * zeroth + b * last + c * before_last, a * first + b * zeroth + c * last

    key0, key1 = firsts(1, 0, 4)
    value0, value1 = firsts(2, 2, 6)
    product0, product1 = key0 * value0, key1 * value1
    for k, array in enumerate((product0, product1)):
        firsts_ref[pl.ds(k * blocks, blocks), :] = array
    own_product0, own_product1 = (firsts_ref[pl.ds(k * blocks + own, 1), :] for k in range(2))
    before = edge_ref[...].astype(jnp.float32)
    before_last, last = before[EDGE - 2 : EDGE - 1], before[EDGE - 1 : EDGE]
    _, b, c = channel_taps(tables_ref, modes, 0)
    own_query0 = local_ref[pl.ds(0, 1), :] + b * last + c * before_last
    own_query1 = local_ref[pl.ds(1, 1), :] + c * last

    state = jnp.zeros((modes, width), jnp.float32)
    for e in range(blocks - 1):
        end = [recv_ref[e, pl.ds(t * modes, modes), :].astype(jnp.float32) for t in range(tiles)]
        added = (
            jnp.concatenate(end, 1)
            + weight0 * product0[e : e + 1]
            + weight1 * product1[e : e + 1]
        )
        state = jnp.where(e < own, state * over_block + added, state)

    state0 = decay * state + own_product0
    state1 = decay * state0 + own_product1
    gated0, gated1 = (
        q * (jnp.sum(coef * h, 0, keepdims=True) + skip * p)
        for q, h, p in (
            (own_query0, state0, own_product0), (own_query1, state1, own_product1)
        )
    )

    start = coef * (state + grow * (own_product0 + grow * own_product1))
    for j in range(CHUNKS):
        for t in range(width // LANES):
            where = pl.ds(t * modes * CHUNKS + j, modes, stride=CHUNKS)
            states_ref[where, :] = start[:, t * LANES : (t + 1) * LANES]
        start = start * over_chunk
    for t in range(width // LANES):
        part = [spread(decay, r, t) for r in range(modes)]
        begin = tuple(
            states_ref[pl.ds((t * modes + r) * CHUNKS, CHUNKS), :] for r in range(modes)
        )

        def step(i, carry, t=t, part=part):
            carry = tuple(d * h for d, h in zip(part, carry))
            where = pl.ds(t * rows + i, CHUNKS, stride=steps)
            conv_ref[where, :] = functools.reduce(jnp.add, carry)
            return carry

        lax.fori_loop(0, steps, step, begin, unroll=4)
    query, base = local_ref[pl.ds(0, rows), :], local_ref[pl.ds(rows, rows), :]
    gated = base + query * whole(conv_ref, rows, width)
    row = lax.broadcasted_iota(jnp.int32, (rows, width), 0)
    gated = jnp.where(row == 0, gated0, jnp.where(row == 1, gated1, gated))
    gated = gated.astype(jnp.bfloat16).astype(jnp.float32)
    root = jnp.sqrt(jnp.sqrt(jnp.abs(gated) * 2.0**32))
    out_ref[...] = jnp.where(gated < 0.0, -root, root)


def shards(features, short_taps, residues, rates, skip, out_weight):
    blocks = lax.axis_size("ctx")
    rows, _, width = features.shape
    modes = rates.shape[0]
    feats = features.transpose(1, 0, 2)
    skip = skip.reshape(1, width)
    f32 = jnp.float32
    tiles = width // LANES
    payload = tiles * (modes + RIM)
    plane = jax.ShapeDtypeStruct((rows, width), f32)
    by_row = pltpu.VMEM((tiles * rows, LANES), f32)
    by_mode = pltpu.VMEM((tiles * modes * CHUNKS, LANES), f32)
    whole_in = pl.BlockSpec(memory_space=pltpu.VMEM)
    sent, tables = pl.pallas_call(
        state_kernel,
        in_specs=[pl.BlockSpec(memory_space=pltpu.HBM)] * 5,
        out_specs=(whole_in,) * 2,
        out_shape=(
            jax.ShapeDtypeStruct((blocks, payload, LANES), jnp.bfloat16),
            pltpu.VMEM(((TABLES + 1) * modes, width), f32),
        ),
        scratch_shapes=[
            pltpu.VMEM(feats.shape, feats.dtype),
            pltpu.VMEM(short_taps.shape, f32),
            pltpu.VMEM(rates.shape, f32),
            pltpu.VMEM(residues.shape, f32),
            pltpu.VMEM(skip.shape, f32),
            pltpu.SemaphoreType.DMA((5,)),
        ],
        name="block_state",
    )(feats, short_taps, rates, residues, skip)
    received = lax.all_to_all(sent, "ctx", split_axis=0, concat_axis=0, tiled=True)
    local, edge = pl.pallas_call(
        local_kernel,
        in_specs=[whole_in] * 2,
        out_specs=(whole_in,) * 2,
        out_shape=(
            jax.ShapeDtypeStruct((2 * rows + (TABLES + 1) * modes, width), f32),
            jax.ShapeDtypeStruct((EDGE, width), jnp.bfloat16),
        ),
        scratch_shapes=[by_row, by_mode, by_row],
        compiler_params=pltpu.CompilerParams(vmem_limit_bytes=KERNEL_VMEM),
        name="local_conv",
    )(feats, tables)
    before = lax.ppermute(edge, "ctx", [(i, i + 1) for i in range(blocks - 1)])
    coded = pl.pallas_call(
        carry_kernel,
        in_specs=[whole_in] * 3,
        out_specs=whole_in,
        out_shape=plane,
        scratch_shapes=[
            pltpu.VMEM((tiles * blocks * RIM, LANES), f32),
            pltpu.VMEM((2 * blocks, width), f32),
            by_mode,
            by_row,
        ],
        compiler_params=pltpu.CompilerParams(vmem_limit_bytes=KERNEL_VMEM),
        name="carry_gate",
    )(received, before, local)
    gathered = lax.all_gather(coded.astype(jnp.float16), "tp", axis=1, tiled=True).astype(f32)
    square = gathered * gathered
    gated = (square * (gathered * jnp.abs(gathered))).astype(jnp.bfloat16)
    mixed = jnp.dot(gated, out_weight, preferred_element_type=f32)
    return (mixed * 2.0**-32).astype(jnp.bfloat16)


def solution(mesh):
    in_specs = (
        P("ctx", None, "tp"),
        P(None, None, "tp"),
        P(None, "tp"),
        P(None, "tp"),
        P("tp"),
        P(None, "tp"),
    )
    return jax.shard_map(
        shards, mesh=mesh, in_specs=in_specs, out_specs=P("ctx", "tp"), check_vma=False
    )
```

```python
import functools

import jax
import jax.numpy as jnp
from jax import lax
from jax.experimental import pallas as pl
from jax.experimental.pallas import tpu as pltpu
from jax.sharding import PartitionSpec as P

SHORT = 3
CHUNKS = 8
RIM = 8
EDGE = 16
LANES = 128
TABLES = 7
KERNEL_VMEM = 12 * 2**20
HIGHEST = lax.Precision.HIGHEST


def per_channel(table, width):
    filters = table.shape[1]
    group = width // filters
    row = lax.broadcasted_iota(jnp.int32, (filters, width), 0)
    col = lax.broadcasted_iota(jnp.int32, (filters, width), 1)
    pick = jnp.where(col // group == row, 1.0, 0.0).astype(jnp.float32)
    return lax.dot_general(
        table, pick, (((1,), (0,)), ((), ())), precision=HIGHEST,
        preferred_element_type=jnp.float32,
    )


def short_filter(block, taps, before_last, last):
    row = lax.broadcasted_iota(jnp.int32, block.shape, 0)
    one = jnp.where(row == 0, last, pltpu.roll(block, 1, 0))
    two = jnp.where(row == 0, before_last, jnp.where(row == 1, last, pltpu.roll(block, 2, 0)))
    return taps[0] * block + taps[1] * one + taps[2] * two


def save(ref, array):
    rows, width = array.shape
    for t in range(width // LANES):
        ref[pl.ds(t * rows, rows), :] = array[:, t * LANES : (t + 1) * LANES]


def strided(ref, rows, width, start, count, stride):
    return jnp.concatenate(
        [ref[pl.ds(t * rows + start, count, stride=stride), :] for t in range(width // LANES)], 1
    )


def whole(ref, rows, width):
    return jnp.concatenate([ref[pl.ds(t * rows, rows), :] for t in range(width // LANES)], 1)


def spread(table, r, t):
    return jnp.broadcast_to(table[r : r + 1, t * LANES : (t + 1) * LANES], (CHUNKS, LANES))


def recur(product_ref, base, decay, states, steps, visit=None):
    def step(i, carry):
        now = product_ref[pl.ds(base + i, CHUNKS, stride=steps), :]
        carry = tuple(d * h + now for d, h in zip(decay, carry))
        if visit is not None:
            visit(i, carry)
        return carry

    return lax.fori_loop(0, steps, step, states, unroll=16)


def chunk_ends(product_ref, ends_ref, decay, rows):
    modes, width = decay.shape
    for t in range(width // LANES):
        blank = tuple(jnp.zeros((CHUNKS, LANES), jnp.float32) for _ in range(modes))
        part = [spread(decay, r, t) for r in range(modes)]
        ends = recur(product_ref, t * rows, part, blank, rows // CHUNKS)
        for r, end in enumerate(ends):
            ends_ref[pl.ds((t * modes + r) * CHUNKS, CHUNKS), :] = end


def table(tables_ref, modes, k):
    return tables_ref[pl.ds(k * modes, modes), :]


def single(tables_ref, modes, k):
    return tables_ref[pl.ds(TABLES * modes + k, 1), :]


def channel_taps(tables_ref, modes, j):
    return [single(tables_ref, modes, SHORT * j + shift) for shift in range(SHORT)]


def inner_product(feat_ref, tables_ref, modes):
    rows, width = feat_ref.shape[1:]
    zero = jnp.zeros((1, width), jnp.float32)
    keys, values = (
        short_filter(
            feat_ref[j].astype(jnp.float32), channel_taps(tables_ref, modes, j), zero, zero
        )
        for j in (1, 2)
    )
    row = lax.broadcasted_iota(jnp.int32, (rows, width), 0)
    return jnp.where(row < SHORT - 1, 0.0, keys * values)


def split(array):
    head = array.astype(jnp.bfloat16)
    return head, (array - head.astype(jnp.float32)).astype(jnp.bfloat16)


def weigh(left, right):
    return jnp.dot(left, right, preferred_element_type=jnp.float32)


def state_kernel(
    feat_hbm, taps_hbm, rates_hbm, residues_hbm, skip_hbm, send_ref, tables_ref,
    feat_ref, taps_ref, rates_ref, residues_ref, skip_ref, sems,
):
    copies = [
        pltpu.make_async_copy(source, target, sems.at[k])
        for k, (source, target) in enumerate(
            (
                (rates_hbm, rates_ref), (residues_hbm, residues_ref), (taps_hbm, taps_ref),
                (skip_hbm, skip_ref), (feat_hbm, feat_ref),
            )
        )
    ]
    for copy in copies:
        copy.start()
    rows, width = feat_ref.shape[1:]
    modes = rates_ref.shape[0]
    steps = rows // CHUNKS
    copies[0].wait()
    copies[1].wait()
    rates = rates_ref[...]
    lam = per_channel(rates, width)
    decay = jnp.exp(-lam)
    over_chunk = jnp.exp(-lam * float(steps))
    coef = per_channel(residues_ref[...] * jnp.sqrt(2.0 * rates), width)
    for k, values in enumerate(
        (
            decay,
            jnp.exp(lam),
            jnp.exp(-lam * float(rows - 2)),
            jnp.exp(-lam * float(rows - 1)),
            jnp.exp(-lam * float(rows)),
            over_chunk,
            coef,
        )
    ):
        tables_ref[pl.ds(k * modes, modes), :] = values
    filters = rates.shape[1]
    column = jnp.concatenate([rates[:, f : f + 1] for f in range(filters)], 0)
    age = rows - 1 - lax.broadcasted_iota(jnp.int32, (filters * modes, rows), 1)
    weights, weights_rest = split(jnp.exp(-column * age.astype(jnp.float32)))
    copies[2].wait()
    copies[3].wait()
    taps = [taps_ref[shift, j : j + 1, :] for j in range(3) for shift in range(SHORT)]
    unused = [jnp.zeros((modes - 3 * SHORT - 1, width), jnp.float32)]
    tables_ref[pl.ds(TABLES * modes, modes), :] = jnp.concatenate(
        taps + [skip_ref[...]] + unused, 0
    )
    copies[4].wait()
    product, product_rest = split(inner_product(feat_ref, tables_ref, modes))
    every = weigh(weights, product) + (weigh(weights, product_rest) + weigh(weights_rest, product))
    owner = lax.broadcasted_iota(jnp.int32, (modes, width), 1) // (width // filters)
    total = jnp.zeros((modes, width), jnp.float32)
    for f in range(filters):
        total = jnp.where(owner == f, every[f * modes : (f + 1) * modes], total)
    edges = [
        feat_ref[j, pl.ds(first, EDGE), :].astype(jnp.float32)[at : at + 2]
        for first, at in ((0, 0), (rows - EDGE, EDGE - 2))
        for j in (1, 2)
    ]
    edges = jnp.concatenate(edges, 0)
    block = jnp.concatenate(
        [a[:, t * LANES : (t + 1) * LANES] for a in (total, edges) for t in range(width // LANES)], 0
    )
    block = block.astype(jnp.bfloat16)
    for e in range(send_ref.shape[0]):
        send_ref[e] = block


def local_kernel(
    feat_ref, tables_ref, local_ref, edge_ref, product_ref, states_ref, conv_ref
):
    rows, width = feat_ref.shape[1:]
    modes = tables_ref.shape[0] // (TABLES + 1)
    steps = rows // CHUNKS
    decay, over_chunk, coef = (table(tables_ref, modes, k) for k in (0, 5, 6))
    zero = jnp.zeros((1, width), jnp.float32)
    query = short_filter(
        feat_ref[0].astype(jnp.float32), channel_taps(tables_ref, modes, 0), zero, zero
    )
    product = inner_product(feat_ref, tables_ref, modes)
    save(product_ref, product)
    chunk_ends(product_ref, states_ref, decay, rows)
    state = jnp.zeros((modes, width), jnp.float32)
    for j in range(CHUNKS):
        end = strided(states_ref, modes * CHUNKS, width, j, modes, CHUNKS)
        for t in range(width // LANES):
            where = pl.ds(t * modes * CHUNKS + j, modes, stride=CHUNKS)
            states_ref[where, :] = state[:, t * LANES : (t + 1) * LANES]
        state = state * over_chunk + end
    for t in range(width // LANES):
        part = [spread(decay, r, t) for r in range(modes)]
        scale = [spread(coef, r, t) for r in range(modes)]
        begin = tuple(
            states_ref[pl.ds((t * modes + r) * CHUNKS, CHUNKS), :] for r in range(modes)
        )

        def visit(i, carry, t=t, scale=scale):
            total = functools.reduce(jnp.add, [s * h for s, h in zip(scale, carry)])
            conv_ref[pl.ds(t * rows + i, CHUNKS, stride=steps), :] = total

        recur(product_ref, t * rows, part, begin, steps, visit)
    skip = single(tables_ref, modes, 3 * SHORT)
    local_ref[pl.ds(2 * rows, (TABLES + 1) * modes), :] = tables_ref[...]
    edge_ref[...] = feat_ref[0, pl.ds(rows - EDGE, EDGE), :]
    local_ref[pl.ds(0, rows), :] = query
    local_ref[pl.ds(rows, rows), :] = query * (whole(conv_ref, rows, width) + skip * product)


def carry_kernel(
    recv_ref, edge_ref, local_ref, out_ref,
    rims_ref, firsts_ref, states_ref, conv_ref,
):
    blocks = recv_ref.shape[0]
    rows, width = out_ref.shape
    tiles = width // LANES
    modes = recv_ref.shape[1] // tiles - RIM
    steps = rows // CHUNKS
    own = lax.axis_index("ctx")
    tables_ref = local_ref.at[pl.ds(2 * rows, (TABLES + 1) * modes)]
    decay, grow, weight1, weight0, over_block, over_chunk, coef = (
        table(tables_ref, modes, k) for k in range(TABLES)
    )
    skip = single(tables_ref, modes, 3 * SHORT)

    for e in range(blocks):
        edges = recv_ref[e, pl.ds(tiles * modes, tiles * RIM), :].astype(jnp.float32)
        rims_ref[pl.ds(e * tiles * RIM, tiles * RIM), :] = edges

    def edge(k):
        return strided(rims_ref, RIM, width, k, blocks, tiles * RIM)

    block_row = lax.broadcasted_iota(jnp.int32, (blocks, width), 0)

    def earlier(k):
        return jnp.where(block_row == 0, 0.0, pltpu.roll(edge(k), 1, 0))

    def firsts(j, head, tail):
        zeroth, first = edge(head), edge(head + 1)
        before_last, last = earlier(tail), earlier(tail + 1)
        a, b, c = channel_taps(tables_ref, modes, j)
        return a * zeroth + b * last + c * before_last, a * first + b * zeroth + c * last

    key0, key1 = firsts(1, 0, 4)
    value0, value1 = firsts(2, 2, 6)
    product0, product1 = key0 * value0, key1 * value1
    for k, array in enumerate((product0, product1)):
        firsts_ref[pl.ds(k * blocks, blocks), :] = array
    own_product0, own_product1 = (firsts_ref[pl.ds(k * blocks + own, 1), :] for k in range(2))
    before = edge_ref[...].astype(jnp.float32)
    before_last, last = before[EDGE - 2 : EDGE - 1], before[EDGE - 1 : EDGE]
    _, b, c = channel_taps(tables_ref, modes, 0)
    own_query0 = local_ref[pl.ds(0, 1), :] + b * last + c * before_last
    own_query1 = local_ref[pl.ds(1, 1), :] + c * last

    state = jnp.zeros((modes, width), jnp.float32)
    for e in range(blocks - 1):
        end = [recv_ref[e, pl.ds(t * modes, modes), :].astype(jnp.float32) for t in range(tiles)]
        added = (
            jnp.concatenate(end, 1)
            + weight0 * product0[e : e + 1]
            + weight1 * product1[e : e + 1]
        )
        state = jnp.where(e < own, state * over_block + added, state)

    state0 = decay * state + own_product0
    state1 = decay * state0 + own_product1
    gated0, gated1 = (
        q * (jnp.sum(coef * h, 0, keepdims=True) + skip * p)
        for q, h, p in (
            (own_query0, state0, own_product0), (own_query1, state1, own_product1)
        )
    )

    start = coef * (state + grow * (own_product0 + grow * own_product1))
    for j in range(CHUNKS):
        for t in range(width // LANES):
            where = pl.ds(t * modes * CHUNKS + j, modes, stride=CHUNKS)
            states_ref[where, :] = start[:, t * LANES : (t + 1) * LANES]
        start = start * over_chunk
    for t in range(width // LANES):
        part = [spread(decay, r, t) for r in range(modes)]
        begin = tuple(
            states_ref[pl.ds((t * modes + r) * CHUNKS, CHUNKS), :] for r in range(modes)
        )

        def step(i, carry, t=t, part=part):
            carry = tuple(d * h for d, h in zip(part, carry))
            where = pl.ds(t * rows + i, CHUNKS, stride=steps)
            conv_ref[where, :] = functools.reduce(jnp.add, carry)
            return carry

        lax.fori_loop(0, steps, step, begin, unroll=16)
    query, base = local_ref[pl.ds(0, rows), :], local_ref[pl.ds(rows, rows), :]
    gated = base + query * whole(conv_ref, rows, width)
    row = lax.broadcasted_iota(jnp.int32, (rows, width), 0)
    gated = jnp.where(row == 0, gated0, jnp.where(row == 1, gated1, gated))
    gated = gated.astype(jnp.bfloat16).astype(jnp.float32)
    root = jnp.sqrt(jnp.sqrt(jnp.abs(gated) * 2.0**32))
    out_ref[...] = jnp.where(gated < 0.0, -root, root)


def shards(features, short_taps, residues, rates, skip, out_weight):
    blocks = lax.axis_size("ctx")
    rows, _, width = features.shape
    modes = rates.shape[0]
    feats = features.transpose(1, 0, 2)
    skip = skip.reshape(1, width)
    f32 = jnp.float32
    tiles = width // LANES
    payload = tiles * (modes + RIM)
    plane = jax.ShapeDtypeStruct((rows, width), f32)
    by_row = pltpu.VMEM((tiles * rows, LANES), f32)
    by_mode = pltpu.VMEM((tiles * modes * CHUNKS, LANES), f32)
    whole_in = pl.BlockSpec(memory_space=pltpu.VMEM)
    sent, tables = pl.pallas_call(
        state_kernel,
        in_specs=[pl.BlockSpec(memory_space=pltpu.HBM)] * 5,
        out_specs=(whole_in,) * 2,
        out_shape=(
            jax.ShapeDtypeStruct((blocks, payload, LANES), jnp.bfloat16),
            pltpu.VMEM(((TABLES + 1) * modes, width), f32),
        ),
        scratch_shapes=[
            pltpu.VMEM(feats.shape, feats.dtype),
            pltpu.VMEM(short_taps.shape, f32),
            pltpu.VMEM(rates.shape, f32),
            pltpu.VMEM(residues.shape, f32),
            pltpu.VMEM(skip.shape, f32),
            pltpu.SemaphoreType.DMA((5,)),
        ],
        name="block_state",
    )(feats, short_taps, rates, residues, skip)
    received = lax.all_to_all(sent, "ctx", split_axis=0, concat_axis=0, tiled=True)
    local, edge = pl.pallas_call(
        local_kernel,
        in_specs=[whole_in] * 2,
        out_specs=(whole_in,) * 2,
        out_shape=(
            jax.ShapeDtypeStruct((2 * rows + (TABLES + 1) * modes, width), f32),
            jax.ShapeDtypeStruct((EDGE, width), jnp.bfloat16),
        ),
        scratch_shapes=[by_row, by_mode, by_row],
        compiler_params=pltpu.CompilerParams(vmem_limit_bytes=KERNEL_VMEM),
        name="local_conv",
    )(feats, tables)
    before = lax.ppermute(edge, "ctx", [(i, i + 1) for i in range(blocks - 1)])
    coded = pl.pallas_call(
        carry_kernel,
        in_specs=[whole_in] * 3,
        out_specs=whole_in,
        out_shape=plane,
        scratch_shapes=[
            pltpu.VMEM((tiles * blocks * RIM, LANES), f32),
            pltpu.VMEM((2 * blocks, width), f32),
            by_mode,
            by_row,
        ],
        compiler_params=pltpu.CompilerParams(vmem_limit_bytes=KERNEL_VMEM),
        name="carry_gate",
    )(received, before, local)
    gathered = lax.all_gather(coded.astype(jnp.float16), "tp", axis=1, tiled=True).astype(f32)
    square = gathered * gathered
    gated = (square * (gathered * jnp.abs(gathered))).astype(jnp.bfloat16)
    mixed = jnp.dot(gated, out_weight, preferred_element_type=f32)
    return (mixed * 2.0**-32).astype(jnp.bfloat16)


def solution(mesh):
    in_specs = (
        P("ctx", None, "tp"),
        P(None, None, "tp"),
        P(None, "tp"),
        P(None, "tp"),
        P("tp"),
        P(None, "tp"),
    )
    return jax.shard_map(
        shards, mesh=mesh, in_specs=in_specs, out_specs=P("ctx", "tp"), check_vma=False
    )
```

```python
import functools

import jax
import jax.numpy as jnp
from jax import lax
from jax.experimental import pallas as pl
from jax.experimental.pallas import tpu as pltpu
from jax.sharding import PartitionSpec as P

SHORT = 3
CHUNKS = 8
RIM = 8
EDGE = 16
LANES = 128
TABLES = 7
KERNEL_VMEM = 12 * 2**20
HIGHEST = lax.Precision.HIGHEST


def per_channel(table, width):
    filters = table.shape[1]
    group = width // filters
    row = lax.broadcasted_iota(jnp.int32, (filters, width), 0)
    col = lax.broadcasted_iota(jnp.int32, (filters, width), 1)
    pick = jnp.where(col // group == row, 1.0, 0.0).astype(jnp.float32)
    return lax.dot_general(
        table, pick, (((1,), (0,)), ((), ())), precision=HIGHEST,
        preferred_element_type=jnp.float32,
    )


def short_filter(block, taps, before_last, last):
    row = lax.broadcasted_iota(jnp.int32, block.shape, 0)
    one = jnp.where(row == 0, last, pltpu.roll(block, 1, 0))
    two = jnp.where(row == 0, before_last, jnp.where(row == 1, last, pltpu.roll(block, 2, 0)))
    return taps[0] * block + taps[1] * one + taps[2] * two


def save(ref, array):
    rows, width = array.shape
    for t in range(width // LANES):
        ref[pl.ds(t * rows, rows), :] = array[:, t * LANES : (t + 1) * LANES]


def strided(ref, rows, width, start, count, stride):
    return jnp.concatenate(
        [ref[pl.ds(t * rows + start, count, stride=stride), :] for t in range(width // LANES)], 1
    )


def whole(ref, rows, width):
    return jnp.concatenate([ref[pl.ds(t * rows, rows), :] for t in range(width // LANES)], 1)


def spread(table, r, t):
    return jnp.broadcast_to(table[r : r + 1, t * LANES : (t + 1) * LANES], (CHUNKS, LANES))


def recur(product_ref, base, decay, states, steps, visit=None):
    def step(i, carry):
        now = product_ref[pl.ds(base + i, CHUNKS, stride=steps), :]
        carry = tuple(d * h + now for d, h in zip(decay, carry))
        if visit is not None:
            visit(i, carry)
        return carry

    return lax.fori_loop(0, steps, step, states, unroll=16)


def chunk_ends(product_ref, ends_ref, decay, rows):
    modes, width = decay.shape
    for t in range(width // LANES):
        blank = tuple(jnp.zeros((CHUNKS, LANES), jnp.float32) for _ in range(modes))
        part = [spread(decay, r, t) for r in range(modes)]
        ends = recur(product_ref, t * rows, part, blank, rows // CHUNKS)
        for r, end in enumerate(ends):
            ends_ref[pl.ds((t * modes + r) * CHUNKS, CHUNKS), :] = end


def table(tables_ref, modes, k):
    return tables_ref[pl.ds(k * modes, modes), :]


def single(tables_ref, modes, k):
    return tables_ref[pl.ds(TABLES * modes + k, 1), :]


def channel_taps(tables_ref, modes, j):
    return [single(tables_ref, modes, SHORT * j + shift) for shift in range(SHORT)]


def inner_product(feat_ref, tables_ref, modes):
    rows, width = feat_ref.shape[1:]
    zero = jnp.zeros((1, width), jnp.float32)
    keys, values = (
        short_filter(
            feat_ref[j].astype(jnp.float32), channel_taps(tables_ref, modes, j), zero, zero
        )
        for j in (1, 2)
    )
    row = lax.broadcasted_iota(jnp.int32, (rows, width), 0)
    return jnp.where(row < SHORT - 1, 0.0, keys * values)


def split(array):
    head = array.astype(jnp.bfloat16)
    return head, (array - head.astype(jnp.float32)).astype(jnp.bfloat16)


def weigh(left, right):
    return jnp.dot(left, right, preferred_element_type=jnp.float32)


def state_kernel(
    feat_hbm, taps_hbm, rates_hbm, residues_hbm, skip_hbm, send_ref, tables_ref,
    feat_ref, taps_ref, rates_ref, residues_ref, skip_ref, sems,
):
    copies = [
        pltpu.make_async_copy(source, target, sems.at[k])
        for k, (source, target) in enumerate(
            (
                (rates_hbm, rates_ref), (residues_hbm, residues_ref), (taps_hbm, taps_ref),
                (skip_hbm, skip_ref), (feat_hbm.at[pl.ds(1, 2)], feat_ref.at[pl.ds(1, 2)]),
            )
        )
    ]
    for copy in copies:
        copy.start()
    rows, width = feat_ref.shape[1:]
    modes = rates_ref.shape[0]
    steps = rows // CHUNKS
    copies[0].wait()
    copies[1].wait()
    rates = rates_ref[...]
    lam = per_channel(rates, width)
    decay = jnp.exp(-lam)
    over_chunk = jnp.exp(-lam * float(steps))
    coef = per_channel(residues_ref[...] * jnp.sqrt(2.0 * rates), width)
    for k, values in enumerate(
        (
            decay,
            jnp.exp(lam),
            jnp.exp(-lam * float(rows - 2)),
            jnp.exp(-lam * float(rows - 1)),
            jnp.exp(-lam * float(rows)),
            over_chunk,
            coef,
        )
    ):
        tables_ref[pl.ds(k * modes, modes), :] = values
    filters = rates.shape[1]
    column = jnp.concatenate([rates[:, f : f + 1] for f in range(filters)], 0)
    age = rows - 1 - lax.broadcasted_iota(jnp.int32, (filters * modes, rows), 1)
    weights, weights_rest = split(jnp.exp(-column * age.astype(jnp.float32)))
    copies[2].wait()
    copies[3].wait()
    taps = [taps_ref[shift, j : j + 1, :] for j in range(3) for shift in range(SHORT)]
    unused = [jnp.zeros((modes - 3 * SHORT - 1, width), jnp.float32)]
    tables_ref[pl.ds(TABLES * modes, modes), :] = jnp.concatenate(
        taps + [skip_ref[...]] + unused, 0
    )
    copies[4].wait()
    product, product_rest = split(inner_product(feat_ref, tables_ref, modes))
    every = weigh(weights, product) + (weigh(weights, product_rest) + weigh(weights_rest, product))
    owner = lax.broadcasted_iota(jnp.int32, (modes, width), 1) // (width // filters)
    total = jnp.zeros((modes, width), jnp.float32)
    for f in range(filters):
        total = jnp.where(owner == f, every[f * modes : (f + 1) * modes], total)
    edges = [
        feat_ref[j, pl.ds(first, EDGE), :].astype(jnp.float32)[at : at + 2]
        for first, at in ((0, 0), (rows - EDGE, EDGE - 2))
        for j in (1, 2)
    ]
    edges = jnp.concatenate(edges, 0)
    block = jnp.concatenate(
        [a[:, t * LANES : (t + 1) * LANES] for a in (total, edges) for t in range(width // LANES)], 0
    )
    block = block.astype(jnp.bfloat16)
    for e in range(send_ref.shape[0]):
        send_ref[e] = block


def local_kernel(
    feat_ref, tables_ref, local_ref, edge_ref, product_ref, states_ref, conv_ref
):
    rows, width = feat_ref.shape[1:]
    modes = tables_ref.shape[0] // (TABLES + 1)
    steps = rows // CHUNKS
    decay, over_chunk, coef = (table(tables_ref, modes, k) for k in (0, 5, 6))
    zero = jnp.zeros((1, width), jnp.float32)
    query = short_filter(
        feat_ref[0].astype(jnp.float32), channel_taps(tables_ref, modes, 0), zero, zero
    )
    product = inner_product(feat_ref, tables_ref, modes)
    save(product_ref, product)
    chunk_ends(product_ref, states_ref, decay, rows)
    state = jnp.zeros((modes, width), jnp.float32)
    for j in range(CHUNKS):
        end = strided(states_ref, modes * CHUNKS, width, j, modes, CHUNKS)
        for t in range(width // LANES):
            where = pl.ds(t * modes * CHUNKS + j, modes, stride=CHUNKS)
            states_ref[where, :] = state[:, t * LANES : (t + 1) * LANES]
        state = state * over_chunk + end
    for t in range(width // LANES):
        part = [spread(decay, r, t) for r in range(modes)]
        scale = [spread(coef, r, t) for r in range(modes)]
        begin = tuple(
            states_ref[pl.ds((t * modes + r) * CHUNKS, CHUNKS), :] for r in range(modes)
        )

        def visit(i, carry, t=t, scale=scale):
            total = functools.reduce(jnp.add, [s * h for s, h in zip(scale, carry)])
            conv_ref[pl.ds(t * rows + i, CHUNKS, stride=steps), :] = total

        recur(product_ref, t * rows, part, begin, steps, visit)
    skip = single(tables_ref, modes, 3 * SHORT)
    local_ref[pl.ds(2 * rows, (TABLES + 1) * modes), :] = tables_ref[...]
    edge_ref[...] = feat_ref[0, pl.ds(rows - EDGE, EDGE), :]
    local_ref[pl.ds(0, rows), :] = query
    local_ref[pl.ds(rows, rows), :] = query * (whole(conv_ref, rows, width) + skip * product)


def carry_kernel(
    recv_ref, edge_ref, local_ref, out_ref,
    rims_ref, firsts_ref, states_ref, conv_ref,
):
    blocks = recv_ref.shape[0]
    rows, width = out_ref.shape
    tiles = width // LANES
    modes = recv_ref.shape[1] // tiles - RIM
    steps = rows // CHUNKS
    own = lax.axis_index("ctx")
    tables_ref = local_ref.at[pl.ds(2 * rows, (TABLES + 1) * modes)]
    decay, grow, weight1, weight0, over_block, over_chunk, coef = (
        table(tables_ref, modes, k) for k in range(TABLES)
    )
    skip = single(tables_ref, modes, 3 * SHORT)

    for e in range(blocks):
        edges = recv_ref[e, pl.ds(tiles * modes, tiles * RIM), :].astype(jnp.float32)
        rims_ref[pl.ds(e * tiles * RIM, tiles * RIM), :] = edges

    def edge(k):
        return strided(rims_ref, RIM, width, k, blocks, tiles * RIM)

    block_row = lax.broadcasted_iota(jnp.int32, (blocks, width), 0)

    def earlier(k):
        return jnp.where(block_row == 0, 0.0, pltpu.roll(edge(k), 1, 0))

    def firsts(j, head, tail):
        zeroth, first = edge(head), edge(head + 1)
        before_last, last = earlier(tail), earlier(tail + 1)
        a, b, c = channel_taps(tables_ref, modes, j)
        return a * zeroth + b * last + c * before_last, a * first + b * zeroth + c * last

    key0, key1 = firsts(1, 0, 4)
    value0, value1 = firsts(2, 2, 6)
    product0, product1 = key0 * value0, key1 * value1
    for k, array in enumerate((product0, product1)):
        firsts_ref[pl.ds(k * blocks, blocks), :] = array
    own_product0, own_product1 = (firsts_ref[pl.ds(k * blocks + own, 1), :] for k in range(2))
    before = edge_ref[...].astype(jnp.float32)
    before_last, last = before[EDGE - 2 : EDGE - 1], before[EDGE - 1 : EDGE]
    _, b, c = channel_taps(tables_ref, modes, 0)
    own_query0 = local_ref[pl.ds(0, 1), :] + b * last + c * before_last
    own_query1 = local_ref[pl.ds(1, 1), :] + c * last

    state = jnp.zeros((modes, width), jnp.float32)
    for e in range(blocks - 1):
        end = [recv_ref[e, pl.ds(t * modes, modes), :].astype(jnp.float32) for t in range(tiles)]
        added = (
            jnp.concatenate(end, 1)
            + weight0 * product0[e : e + 1]
            + weight1 * product1[e : e + 1]
        )
        state = jnp.where(e < own, state * over_block + added, state)

    state0 = decay * state + own_product0
    state1 = decay * state0 + own_product1
    gated0, gated1 = (
        q * (jnp.sum(coef * h, 0, keepdims=True) + skip * p)
        for q, h, p in (
            (own_query0, state0, own_product0), (own_query1, state1, own_product1)
        )
    )

    start = coef * (state + grow * (own_product0 + grow * own_product1))
    for j in range(CHUNKS):
        for t in range(width // LANES):
            where = pl.ds(t * modes * CHUNKS + j, modes, stride=CHUNKS)
            states_ref[where, :] = start[:, t * LANES : (t + 1) * LANES]
        start = start * over_chunk
    for t in range(width // LANES):
        part = [spread(decay, r, t) for r in range(modes)]
        begin = tuple(
            states_ref[pl.ds((t * modes + r) * CHUNKS, CHUNKS), :] for r in range(modes)
        )

        def step(i, carry, t=t, part=part):
            carry = tuple(d * h for d, h in zip(part, carry))
            where = pl.ds(t * rows + i, CHUNKS, stride=steps)
            conv_ref[where, :] = functools.reduce(jnp.add, carry)
            return carry

        lax.fori_loop(0, steps, step, begin, unroll=4)
    query, base = local_ref[pl.ds(0, rows), :], local_ref[pl.ds(rows, rows), :]
    gated = base + query * whole(conv_ref, rows, width)
    row = lax.broadcasted_iota(jnp.int32, (rows, width), 0)
    gated = jnp.where(row == 0, gated0, jnp.where(row == 1, gated1, gated))
    gated = gated.astype(jnp.bfloat16).astype(jnp.float32)
    root = jnp.sqrt(jnp.sqrt(jnp.abs(gated) * 2.0**32))
    out_ref[...] = jnp.where(gated < 0.0, -root, root)


def shards(features, short_taps, residues, rates, skip, out_weight):
    blocks = lax.axis_size("ctx")
    rows, _, width = features.shape
    modes = rates.shape[0]
    feats = features.transpose(1, 0, 2)
    skip = skip.reshape(1, width)
    f32 = jnp.float32
    tiles = width // LANES
    payload = tiles * (modes + RIM)
    plane = jax.ShapeDtypeStruct((rows, width), f32)
    by_row = pltpu.VMEM((tiles * rows, LANES), f32)
    by_mode = pltpu.VMEM((tiles * modes * CHUNKS, LANES), f32)
    whole_in = pl.BlockSpec(memory_space=pltpu.VMEM)
    sent, tables = pl.pallas_call(
        state_kernel,
        in_specs=[pl.BlockSpec(memory_space=pltpu.HBM)] * 5,
        out_specs=(whole_in,) * 2,
        out_shape=(
            jax.ShapeDtypeStruct((blocks, payload, LANES), jnp.bfloat16),
            pltpu.VMEM(((TABLES + 1) * modes, width), f32),
        ),
        scratch_shapes=[
            pltpu.VMEM(feats.shape, feats.dtype),
            pltpu.VMEM(short_taps.shape, f32),
            pltpu.VMEM(rates.shape, f32),
            pltpu.VMEM(residues.shape, f32),
            pltpu.VMEM(skip.shape, f32),
            pltpu.SemaphoreType.DMA((5,)),
        ],
        name="block_state",
    )(feats, short_taps, rates, residues, skip)
    received = lax.all_to_all(sent, "ctx", split_axis=0, concat_axis=0, tiled=True)
    local, edge = pl.pallas_call(
        local_kernel,
        in_specs=[whole_in] * 2,
        out_specs=(whole_in,) * 2,
        out_shape=(
            jax.ShapeDtypeStruct((2 * rows + (TABLES + 1) * modes, width), f32),
            jax.ShapeDtypeStruct((EDGE, width), jnp.bfloat16),
        ),
        scratch_shapes=[by_row, by_mode, by_row],
        compiler_params=pltpu.CompilerParams(vmem_limit_bytes=KERNEL_VMEM),
        name="local_conv",
    )(feats, tables)
    before = lax.ppermute(edge, "ctx", [(i, i + 1) for i in range(blocks - 1)])
    coded = pl.pallas_call(
        carry_kernel,
        in_specs=[whole_in] * 3,
        out_specs=whole_in,
        out_shape=plane,
        scratch_shapes=[
            pltpu.VMEM((tiles * blocks * RIM, LANES), f32),
            pltpu.VMEM((2 * blocks, width), f32),
            by_mode,
            by_row,
        ],
        compiler_params=pltpu.CompilerParams(vmem_limit_bytes=KERNEL_VMEM),
        name="carry_gate",
    )(received, before, local)
    gathered = lax.all_gather(coded.astype(jnp.float16), "tp", axis=1, tiled=True).astype(f32)
    square = gathered * gathered
    gated = (square * (gathered * jnp.abs(gathered))).astype(jnp.bfloat16)
    mixed = jnp.dot(gated, out_weight, preferred_element_type=f32)
    return (mixed * 2.0**-32).astype(jnp.bfloat16)


def solution(mesh):
    in_specs = (
        P("ctx", None, "tp"),
        P(None, None, "tp"),
        P(None, "tp"),
        P(None, "tp"),
        P("tp"),
        P(None, "tp"),
    )
    return jax.shard_map(
        shards, mesh=mesh, in_specs=in_specs, out_specs=P("ctx", "tp"), check_vma=False
    )
```
